32 devices in a mesh: dp: 8 (over z, y), expert: 4 (over x, core).
Axes of the slice: x: 2, y: 2, z: 4, core: 2. Of those that a mesh axis runs over, the one named last changes fastest.
Arguments:
- tokens: bfloat16 [8192, 1024], P(('dp', 'expert')), may hold values from -6 to 6
- out_grad: bfloat16 [8192, 1024], P(('dp', 'expert')), may hold values from -3 to 3
- gate_prob: bfloat16 [8192], P(('dp', 'expert')), may hold values from 0.19921875 to 1
- expert_id: int32 [8192], P(('dp', 'expert')), may hold values from 0 to 3, as said below
- up_weight: bfloat16 [4, 1024, 2048], P('expert'), may hold values from -0.1875 to 0.1875
- down_weight: bfloat16 [4, 2048, 1024], P('expert'), may hold values from -0.125 to 0.125
Outputs:
- tokens_grad: bfloat16 [8192, 1024], P(('dp', 'expert'))
- gate_grad: bfloat16 [8192], P(('dp', 'expert'))
- up_weight_grad: float32 [4, 1024, 2048], P('expert', 'dp')
- down_weight_grad: float32 [4, 2048, 1024], P('expert', 'dp')
The draws below stay inside these ranges and needn't reach their ends.
Inputs may be any that keep to these rules, and one draw needn't show every extreme that they name: `expert_id`: among the 256 tokens of one device each expert is named at most 128 times; in every data group one expert is named exactly 128 times by every device of the group.
All inputs are finite; a program needn't handle non-finite values.
Results may differ from the reference program's by a relative error of at most 0.017.
Values may be sent and summed in bfloat16 or wider, within the bound.
No kernel may reach another device: no remote copies, remote signals or barrier semaphores. Data moves between devices by JAX's collectives and lax.ppermute only.
A program may use at most 64 MiB of HBM per device.

```python
import jax
import jax.numpy as jnp
from jax import lax

D = 1024
FF = 2048
EXP_DEV = 1
EXPERTS = 4
TOK_DEV = 256
CAP = 128
TOKENS = 8192
N_DP = 8
N_EXPERT = 4


def draw_expert_id(key, part):
    blocks = TOKENS // TOK_DEV
    group_size = EXPERTS // EXP_DEV
    groups = blocks // group_size
    remaining = TOK_DEV - CAP
    key_hot, key_blocks = jax.random.split(jax.random.fold_in(key, 17))
    hot_groups = jax.random.randint(key_hot, (groups,), 0, EXPERTS).astype(jnp.int32)
    hot_blocks = jnp.repeat(hot_groups, group_size)
    pool_offset = jnp.repeat(jnp.arange(1, EXPERTS, dtype=jnp.int32), CAP)
    block_keys = jax.random.split(key_blocks, blocks)

    def one_block(block_key, hot_expert):
        key_pool, key_rows = jax.random.split(block_key)
        shuffle = jax.random.permutation(key_pool, pool_offset.shape[0])
        others = (hot_expert + pool_offset[shuffle[:remaining]]) % EXPERTS
        labels = jnp.concatenate([jnp.full((CAP,), hot_expert, jnp.int32), others.astype(jnp.int32)])
        return labels[jax.random.permutation(key_rows, TOK_DEV)]
    return jax.vmap(one_block)(block_keys, hot_blocks).reshape(TOKENS).astype(jnp.int32)


def shard_levels(rng, dims, cuts, smallest, high):
    gain = 1.0
    for dim, parts in cuts:
        draws = jax.random.uniform(jax.random.fold_in(jax.random.fold_in(rng, 6), dim), (parts,), jnp.float32, smallest / len(cuts), high / len(cuts))
        gain = gain * jnp.repeat(jnp.exp(draws), dims[dim] // parts).reshape((-1,) + (1,) * (len(dims) - 1 - dim))
    return gain


def gaussian(own_key, shape, width, bound, cuts=(), held_as=jnp.bfloat16):
    gain = shard_levels(own_key, shape, cuts, -0.22, 0.18) if cuts else 1.0
    result = jax.random.normal(own_key, shape, jnp.float32) * width * gain
    return jnp.minimum(jnp.maximum(result, -bound), bound).astype(held_as)


def setup_inputs(seed: int = 0) -> dict:
    key_of = jax.random.split(jax.random.key(seed), 7)
    return {
        "tokens": gaussian(key_of[0], (TOKENS, D), 1.0, 6.0, ((0, 32),)),
        "out_grad": gaussian(key_of[1], (TOKENS, D), 0.5, 3.0, ((0, 32),)),
        "gate_prob": jnp.clip(0.19921875 + 0.80078125 * jax.random.uniform(key_of[2], (TOKENS,), jnp.float32) ** shard_levels(key_of[2], (TOKENS,), ((0, 32),), -0.2, 0.2), 0.19921875, 1.0).astype(jnp.bfloat16),
        "expert_id": draw_expert_id(jax.random.fold_in(key_of[6], 71), 0),
        "up_weight": gaussian(key_of[4], (EXPERTS, D, FF), D ** -0.5, 0.1875, ((0, 4),)),
        "down_weight": gaussian(key_of[5], (EXPERTS, FF, D), FF ** -0.5, 0.125, ((0, 4),)),
    }


SQRT_HALF = 0.7071067811865476
INV_ROOT_TAU = 0.3989422804014327


def gelu_value(pre_act):
    return 0.5 * pre_act * (1.0 + jax.scipy.special.erf(pre_act * SQRT_HALF))


def gelu_slope(pre_act):
    normal_cdf = 0.5 * (1.0 + jax.scipy.special.erf(pre_act * SQRT_HALF))
    return normal_cdf + pre_act * jnp.exp(-0.5 * pre_act * pre_act) * INV_ROOT_TAU


def contract_rows(left, right):
    return lax.dot_general(left.astype(jnp.float32), right.astype(jnp.float32), (((0,), (0,)), ((), ())), preferred_element_type=jnp.float32)


def expert_rows(feat_rows, grad_rows, gate_rows, up_matrix, down_matrix):
    pre_act = jnp.dot(feat_rows, up_matrix, preferred_element_type=jnp.float32)
    hidden = gelu_value(pre_act).astype(jnp.bfloat16)
    expert_out = jnp.dot(hidden, down_matrix, preferred_element_type=jnp.float32)
    gate_grad = jnp.sum(grad_rows.astype(jnp.float32) * expert_out, axis=1).astype(jnp.bfloat16)
    scaled = (gate_rows.astype(jnp.float32)[:, None] * grad_rows.astype(jnp.float32)).astype(jnp.bfloat16)
    hidden_grad = jnp.dot(scaled, down_matrix.T, preferred_element_type=jnp.float32)
    pre_grad = (hidden_grad * gelu_slope(pre_act)).astype(jnp.bfloat16)
    feat_grad = jnp.dot(pre_grad, up_matrix.T, preferred_element_type=jnp.float32).astype(jnp.bfloat16)
    return feat_grad, gate_grad, hidden, scaled, pre_grad


def reference(tokens, out_grad, gate_prob, expert_id, up_weight, down_weight):
    group_rows = N_EXPERT * TOK_DEV
    slot_total = N_EXPERT * CAP
    feat_groups = tokens.reshape(N_DP, group_rows, D)
    grad_groups = out_grad.reshape(N_DP, group_rows, D)
    gate_groups = gate_prob.reshape(N_DP, group_rows)
    label_groups = expert_id.reshape(N_DP, group_rows)

    def per_group(running, inputs):
        up_total, down_total = running
        feat_group, grad_group, gate_group, label_group = inputs

        def per_expert(totals, expert):
            feat_acc, gate_acc = totals
            row_index = jnp.nonzero(label_group == expert, size=slot_total, fill_value=group_rows)[0].astype(jnp.int32)
            feat_rows = jnp.take(feat_group, row_index, axis=0, mode="fill", fill_value=0)
            grad_rows = jnp.take(grad_group, row_index, axis=0, mode="fill", fill_value=0)
            gate_rows = jnp.take(gate_group, row_index, axis=0, mode="fill", fill_value=0)
            feat_grad, gate_grad, hidden, scaled, pre_grad = expert_rows(feat_rows, grad_rows, gate_rows, up_weight[expert], down_weight[expert])
            up_part = lax.optimization_barrier(contract_rows(feat_rows, pre_grad).astype(jnp.bfloat16))
            down_part = lax.optimization_barrier(contract_rows(hidden, scaled).astype(jnp.bfloat16))
            feat_acc = feat_acc.at[row_index].set(feat_grad, mode="drop")
            gate_acc = gate_acc.at[row_index].set(gate_grad, mode="drop")
            return (feat_acc, gate_acc), (up_part, down_part)

        start_acc = (jnp.zeros((group_rows, D), jnp.bfloat16), jnp.zeros((group_rows,), jnp.bfloat16))
        (feat_acc, gate_acc), (up_parts, down_parts) = lax.scan(per_expert, start_acc, jnp.arange(EXPERTS, dtype=jnp.int32))
        return (up_total + up_parts.astype(jnp.float32), down_total + down_parts.astype(jnp.float32)), (feat_acc, gate_acc)

    start_sum = (jnp.zeros((EXPERTS, D, FF), jnp.float32), jnp.zeros((EXPERTS, FF, D), jnp.float32))
    (up_total, down_total), (feat_all, gate_all) = lax.scan(per_group, start_sum, (feat_groups, grad_groups, gate_groups, label_groups))
    divisor = 1.0 / N_DP
    return (feat_all.reshape(TOKENS, D), gate_all.reshape(TOKENS), up_total * divisor, down_total * divisor)
```

```python
import functools

import jax
import jax.numpy as jnp
from jax import lax
from jax.experimental import pallas as pl
from jax.experimental.pallas import tpu as pltpu
from jax.sharding import PartitionSpec as P

SQRT_HALF = 0.7071067811865476
INV_ROOT_TAU = 0.3989422804014327
LANES = 128
VMEM_LIMIT = 40 * 1024 * 1024
F32 = jnp.float32
BF16 = jnp.bfloat16
WHOLE = pl.BlockSpec(memory_space=pltpu.VMEM)


def params(*semantics):
    return pltpu.CompilerParams(
        vmem_limit_bytes=VMEM_LIMIT, dimension_semantics=semantics or None
    )


def dot(left, right, left_dim, right_dim):
    return lax.dot_general(
        left, right, (((left_dim,), (right_dim,)), ((), ())), preferred_element_type=F32
    )


def slot_row(id_row, experts, capacity, me):
    count = id_row.shape[1]
    expert = lax.broadcasted_iota(jnp.int32, (max(experts, 8), count), 0)
    chosen = expert == id_row
    earlier = lax.broadcasted_iota(jnp.int32, (count, count), 0) < lax.broadcasted_iota(
        jnp.int32, (count, count), 1
    )
    before = dot(
        jnp.where(chosen, 1.0, 0.0).astype(BF16), jnp.where(earlier, 1.0, 0.0).astype(BF16), 1, 0
    )
    position = jnp.sum(jnp.where(chosen, before, 0.0), axis=0, keepdims=True).astype(jnp.int32)
    return (id_row ^ me) * capacity + position


def feat_pack_kernel(experts, capacity, me_ref, id_ref, tokens_ref, slot_ref, *outs):
    slot = slot_row(id_ref[...], experts, capacity, me_ref[0])
    slot_ref[...] = slot
    count = slot.shape[1]
    for block, out in enumerate(outs):
        row = lax.broadcasted_iota(jnp.int32, (capacity, count), 0) + block * capacity
        pick = jnp.where(row == slot, 1.0, 0.0).astype(BF16)
        out[...] = dot(pick, tokens_ref[...], 1, 0).astype(BF16)


def grad_pack_kernel(capacity, slot_ref, gate_ref, grad_ref, *outs):
    slot = slot_ref[...]
    gate = gate_ref[...].astype(F32)
    count = slot.shape[1]
    for block, out in enumerate(outs):
        row = lax.broadcasted_iota(jnp.int32, (capacity, count), 0) + block * capacity
        pick = jnp.where(row == slot, gate, 0.0).astype(BF16)
        out[...] = dot(pick, grad_ref[...], 1, 0).astype(BF16)


def unpack_kernel(capacity, width, slot_ref, *refs):
    blocks, (feat_ref, gate_ref) = refs[:-2], refs[-2:]
    slot = slot_ref[...]
    count = slot.shape[1]
    total = None
    for block, ref in enumerate(blocks):
        row = lax.broadcasted_iota(jnp.int32, (capacity, count), 0) + block * capacity
        pick = jnp.where(row == slot, 1.0, 0.0).astype(BF16)
        part = dot(pick, ref[...], 0, 0)
        total = part if total is None else total + part
    feat_ref[...] = total[:, :width].astype(BF16)
    gate_ref[...] = total[:, width:]


def hidden_kernel(*refs):
    *blocks, up_ref, flip_feat_ref, hidden_ref, flip_hidden_ref, slope_ref, feat_ref = refs

    @pl.when(pl.program_id(0) == 0)
    def _():
        feat_ref[...] = jnp.concatenate([ref[...] for ref in blocks], axis=0)
        flip_feat_ref[...] = feat_ref[...].T

    pre_act = dot(feat_ref[...], up_ref[0], 1, 0)
    cdf = 0.5 * (1.0 + lax.erf(pre_act * SQRT_HALF))
    hidden = (pre_act * cdf).astype(BF16)
    hidden_ref[...] = hidden
    flip_hidden_ref[...] = hidden.T
    slope = cdf + pre_act * jnp.exp(-0.5 * pre_act * pre_act) * INV_ROOT_TAU
    slope_ref[...] = slope.astype(BF16)


def pre_grad_kernel(*refs):
    *blocks, down_ref, hidden_ref, slope_ref, pre_ref, sum_ref = refs
    scaled = jnp.concatenate([ref[...] for ref in blocks], axis=0)
    hidden_grad = dot(scaled, down_ref[0], 1, 1)
    pre_ref[...] = (hidden_grad * slope_ref[...].astype(F32)).astype(BF16)
    part = jnp.sum(hidden_grad * hidden_ref[...].astype(F32), axis=1, keepdims=True)

    @pl.when(pl.program_id(0) == 0)
    def _():
        sum_ref[...] = jnp.zeros_like(sum_ref)

    sum_ref[...] += jnp.broadcast_to(part, sum_ref.shape)


def feat_grad_kernel(pre_ref, up_ref, sum_ref, out_ref):
    width = up_ref.shape[1]
    out_ref[:, :width] = dot(pre_ref[...], up_ref[0], 1, 1).astype(BF16)
    total = sum_ref[...]
    high = total.astype(BF16)
    low = (total - high.astype(F32)).astype(BF16)
    lane = lax.broadcasted_iota(jnp.int32, total.shape, 1)
    out_ref[:, width:] = jnp.where(lane == 0, high.astype(F32), low.astype(F32)).astype(BF16)


def feat_grad(pre_grad, up_weight, sums, block, capacity):
    _, width, inner = up_weight.shape
    return pl.pallas_call(
        feat_grad_kernel,
        grid=(1,),
        in_specs=[
            pl.BlockSpec((capacity, inner), lambda i: (block, 0)),
            pl.BlockSpec((1, width, inner), lambda i: (0, 0, 0)),
            pl.BlockSpec((capacity, LANES), lambda i: (block, 0)),
        ],
        out_specs=pl.BlockSpec((capacity, width + LANES), lambda i: (0, 0)),
        out_shape=jax.ShapeDtypeStruct((capacity, width + LANES), BF16),
        compiler_params=params(),
        name="feat_grad",
    )(pre_grad, up_weight, sums)


def ring_index(position, count):
    half = count // 2
    return jnp.where(position < half, 2 * position, 2 * (count - 1 - position) + 1)


def ring_position(index, count):
    return jnp.where(index % 2 == 0, index // 2, count - 1 - index // 2)


def ring_pairs(count):
    half = count // 2
    ring = [2 * p if p < half else 2 * (count - 1 - p) + 1 for p in range(count)]
    return [(ring[p], ring[(p + 1) % count]) for p in range(count)]


def down_kernel(scale, order_ref, fore_ref, back_ref, *refs):
    *blocks, fore_in, back_in = refs[: -1 if scale else -2]
    scaled = jnp.concatenate([ref[...] for ref in blocks], axis=0)
    half = scaled.shape[1] // 2
    fore = dot(fore_ref[...], scaled[:, :half], 1, 0) + fore_in[...].astype(F32)
    back = dot(back_ref[...], scaled[:, half:], 1, 0) + back_in[...].astype(F32)
    if scale:
        refs[-1][0, :, :half] = fore * scale
        refs[-1][0, :, half:] = back * scale
    else:
        refs[-2][...] = fore.astype(BF16)
        refs[-1][...] = back.astype(BF16)


def down_first_kernel(order_ref, fore_ref, back_ref, *refs):
    *blocks, fore_out, back_out = refs
    scaled = jnp.concatenate([ref[...] for ref in blocks], axis=0)
    half = scaled.shape[1] // 2
    fore_out[...] = dot(fore_ref[...], scaled[:, :half], 1, 0).astype(BF16)
    back_out[...] = dot(back_ref[...], scaled[:, half:], 1, 0).astype(BF16)


def up_kernel(scale, order_ref, fore_ref, back_ref, pre_ref, fore_in, back_in, *outs):
    half = pre_ref.shape[1] // 2
    fore = dot(fore_ref[...], pre_ref[:, :half], 1, 0) + fore_in[...].astype(F32)
    back = dot(back_ref[...], pre_ref[:, half:], 1, 0) + back_in[...].astype(F32)
    if scale:
        outs[0][0, :, :half] = fore * scale
        outs[0][0, :, half:] = back * scale
    else:
        outs[0][...] = fore.astype(BF16)
        outs[1][...] = back.astype(BF16)


def up_first_kernel(order_ref, fore_ref, back_ref, pre_ref, fore_out, back_out):
    half = pre_ref.shape[1] // 2
    fore_out[...] = dot(fore_ref[...], pre_ref[:, :half], 1, 0).astype(BF16)
    back_out[...] = dot(back_ref[...], pre_ref[:, half:], 1, 0).astype(BF16)


def ring_step(kernels, name, order, step, count, lefts, rights, arrived):
    first, later = kernels
    rows = lefts.shape[0] // count
    tokens = lefts.shape[1]
    width = rights[0].shape[1]
    last = step == count
    if arrived is None:
        body, arrived = first, ()
    else:
        body = functools.partial(later, 1.0 / count if last else None)
    if last:
        out_specs = pl.BlockSpec((1, rows, width), lambda i, o: (0, 0, 0))
        out_shape = jax.ShapeDtypeStruct((1, rows, width), F32)
    else:
        out_specs = [pl.BlockSpec((rows, width // 2), lambda i, o: (0, 0))] * 2
        out_shape = [jax.ShapeDtypeStruct((rows, width // 2), BF16)] * 2
    full = [pl.BlockSpec(a.shape, lambda i, o: (0, 0)) for a in (*rights, *arrived)]
    return pl.pallas_call(
        body,
        grid_spec=pltpu.PrefetchScalarGridSpec(
            num_scalar_prefetch=1,
            grid=(1,),
            in_specs=[
                pl.BlockSpec((rows, tokens), lambda i, o: (o[0, step - 1], 0)),
                pl.BlockSpec((rows, tokens), lambda i, o: (o[1, step - 1], 0)),
                *full,
            ],
            out_specs=out_specs,
        ),
        out_shape=out_shape,
        compiler_params=params(),
        name=name,
    )(order, lefts, lefts, *rights, *arrived)


def per_device(tokens, out_grad, gate_prob, expert_id, up_weight, down_weight):
    count, width = tokens.shape
    inner = up_weight.shape[2]
    peers = lax.axis_size("expert")
    experts = peers * up_weight.shape[0]
    capacity = 2 * count // experts
    rows = peers * capacity
    ring = lax.axis_size("dp")
    me = lax.axis_index("expert")
    sources = [[(i, i ^ k) for i in range(peers)] for k in range(peers)]
    forward = ring_pairs(ring)
    backward = [(b, a) for a, b in forward]
    place = ring_position(lax.axis_index("dp"), ring)
    steps = jnp.arange(1, ring + 1, dtype=jnp.int32)
    order = ring_index(
        jnp.stack([(place - steps) % ring, (place + steps) % ring]), ring
    ).astype(jnp.int32)

    slot, *feat_out = pl.pallas_call(
        functools.partial(feat_pack_kernel, experts, capacity),
        in_specs=[pl.BlockSpec(memory_space=pltpu.SMEM), WHOLE, WHOLE],
        out_specs=[WHOLE] * (1 + peers),
        out_shape=[jax.ShapeDtypeStruct((1, count), jnp.int32)]
        + [jax.ShapeDtypeStruct((capacity, width), BF16)] * peers,
        compiler_params=params(),
        name="feat_pack",
    )(me.reshape(1), expert_id.reshape(1, count), tokens)
    feat_in = [feat_out[0]] + [
        lax.ppermute(feat_out[k], "expert", sources[k]) for k in reversed(range(1, peers))
    ][::-1]

    grad_out = pl.pallas_call(
        functools.partial(grad_pack_kernel, capacity),
        in_specs=[WHOLE] * 3,
        out_specs=[WHOLE] * peers,
        out_shape=[jax.ShapeDtypeStruct((capacity, width), BF16)] * peers,
        compiler_params=params(),
        name="grad_pack",
    )(slot, gate_prob.reshape(1, count), out_grad)
    grad_in = [grad_out[0]] + [
        lax.ppermute(grad_out[k], "expert", sources[k]) for k in reversed(range(1, peers))
    ][::-1]

    tile = inner // 8
    flip_feat, hidden, flip_hidden, slope = pl.pallas_call(
        hidden_kernel,
        grid=(inner // tile,),
        in_specs=[pl.BlockSpec((capacity, width), lambda i: (0, 0))] * peers
        + [pl.BlockSpec((1, width, tile), lambda i: (0, 0, i))],
        out_specs=[
            pl.BlockSpec((width, rows), lambda i: (0, 0)),
            pl.BlockSpec((rows, tile), lambda i: (0, i)),
            pl.BlockSpec((tile, rows), lambda i: (i, 0)),
            pl.BlockSpec((rows, tile), lambda i: (0, i)),
        ],
        out_shape=[
            jax.ShapeDtypeStruct((width, rows), BF16),
            jax.ShapeDtypeStruct((rows, inner), BF16),
            jax.ShapeDtypeStruct((inner, rows), BF16),
            jax.ShapeDtypeStruct((rows, inner), BF16),
        ],
        scratch_shapes=[pltpu.VMEM((rows, width), BF16)],
        compiler_params=params("arbitrary"),
        name="hidden",
    )(*feat_in, up_weight)

    pre_grad, sums = pl.pallas_call(
        pre_grad_kernel,
        grid=(inner // tile,),
        in_specs=[pl.BlockSpec((capacity, width), lambda i: (0, 0))] * peers
        + [
            pl.BlockSpec((1, tile, width), lambda i: (0, i, 0)),
            pl.BlockSpec((rows, tile), lambda i: (0, i)),
            pl.BlockSpec((rows, tile), lambda i: (0, i)),
        ],
        out_specs=[
            pl.BlockSpec((rows, tile), lambda i: (0, i)),
            pl.BlockSpec((rows, LANES), lambda i: (0, 0)),
        ],
        out_shape=[
            jax.ShapeDtypeStruct((rows, inner), BF16),
            jax.ShapeDtypeStruct((rows, LANES), F32),
        ],
        compiler_params=params("arbitrary"),
        name="pre_grad",
    )(*grad_in, down_weight, hidden, slope)

    down_kernels = (down_first_kernel, down_kernel)
    up_kernels = (up_first_kernel, up_kernel)
    down_arrived = up_arrived = None
    for step in range(1, ring + 1):
        down = ring_step(
            down_kernels, "down_step", order, step, ring, flip_hidden, grad_in, down_arrived
        )
        up = ring_step(
            up_kernels, "up_step", order, step, ring, flip_feat, [pre_grad], up_arrived
        )
        if step < ring:
            down_arrived = (
                lax.ppermute(down[0], "dp", forward),
                lax.ppermute(down[1], "dp", backward),
            )
            up_arrived = (
                lax.ppermute(up[0], "dp", forward),
                lax.ppermute(up[1], "dp", backward),
            )

    feat_back = [feat_grad(pre_grad, up_weight, sums, k, capacity) for k in range(peers)]
    feat_back = [feat_back[0]] + [
        lax.ppermute(feat_back[k], "expert", sources[k]) for k in range(1, peers)
    ]
    tokens_grad, gate_sums = pl.pallas_call(
        functools.partial(unpack_kernel, capacity, width),
        in_specs=[WHOLE] * (1 + peers),
        out_specs=[WHOLE] * 2,
        out_shape=[
            jax.ShapeDtypeStruct((count, width), BF16),
            jax.ShapeDtypeStruct((count, LANES), F32),
        ],
        compiler_params=params(),
        name="unpack",
    )(slot, *feat_back)
    gate_result = ((gate_sums[:, 0] + gate_sums[:, 1]) / gate_prob.astype(F32)).astype(BF16)
    return (tokens_grad, gate_result, up, down)


def solution(mesh):
    return jax.shard_map(
        per_device,
        mesh=mesh,
        in_specs=(
            P(("dp", "expert"), None),
            P(("dp", "expert"), None),
            P(("dp", "expert")),
            P(("dp", "expert")),
            P("expert", None, None),
            P("expert", None, None),
        ),
        out_specs=(
            P(("dp", "expert"), None),
            P(("dp", "expert")),
            P("expert", "dp", None),
            P("expert", "dp", None),
        ),
        check_vma=False,
    )
```

```python
import functools

import jax
import jax.numpy as jnp
from jax import lax
from jax.experimental import pallas as pl
from jax.experimental.pallas import tpu as pltpu
from jax.sharding import PartitionSpec as P

SQRT_HALF = 0.7071067811865476
INV_ROOT_TAU = 0.3989422804014327
LANES = 128
VMEM_LIMIT = 40 * 1024 * 1024
F32 = jnp.float32
BF16 = jnp.bfloat16
WHOLE = pl.BlockSpec(memory_space=pltpu.VMEM)
LATER = pl.BlockSpec(memory_space=pl.ANY)


def in_hbm(array):
    return pltpu.with_memory_space_constraint(array, pltpu.HBM)


def params(*semantics):
    return pltpu.CompilerParams(
        vmem_limit_bytes=VMEM_LIMIT, dimension_semantics=semantics or None
    )


def dot(left, right, left_dim, right_dim):
    return lax.dot_general(
        left, right, (((left_dim,), (right_dim,)), ((), ())), preferred_element_type=F32
    )


def slot_row(id_row, experts, capacity, me):
    count = id_row.shape[1]
    expert = lax.broadcasted_iota(jnp.int32, (max(experts, 8), count), 0)
    chosen = expert == id_row
    earlier = lax.broadcasted_iota(jnp.int32, (count, count), 0) < lax.broadcasted_iota(
        jnp.int32, (count, count), 1
    )
    before = dot(
        jnp.where(chosen, 1.0, 0.0).astype(BF16), jnp.where(earlier, 1.0, 0.0).astype(BF16), 1, 0
    )
    position = jnp.sum(jnp.where(chosen, before, 0.0), axis=0, keepdims=True).astype(jnp.int32)
    return (id_row ^ me) * capacity + position


def pack_kernel(experts, capacity, me_ref, *refs):
    sources, refs = refs[:4], refs[4:]
    slot_ref, outs = refs[0], refs[1:-5]
    held, sems = refs[-5:-1], refs[-1]
    copies = [
        pltpu.make_async_copy(source, target, sems.at[i])
        for i, (source, target) in enumerate(zip(sources, held))
    ]
    for copy in copies:
        copy.start()
    id_ref, tokens_ref, gate_ref, grad_ref = held
    copies[0].wait()
    count = id_ref.shape[0]
    slot = slot_row(id_ref[...].reshape(1, count), experts, capacity, me_ref[0])
    slot_ref[...] = slot
    peers = len(outs) // 2
    copies[1].wait()
    for block in range(peers):
        row = lax.broadcasted_iota(jnp.int32, (capacity, count), 0) + block * capacity
        pick = jnp.where(row == slot, 1.0, 0.0).astype(BF16)
        outs[block][...] = dot(pick, tokens_ref[...], 1, 0).astype(BF16)
    copies[2].wait()
    copies[3].wait()
    gate = gate_ref[...].astype(F32).reshape(1, count)
    for block in range(peers):
        row = lax.broadcasted_iota(jnp.int32, (capacity, count), 0) + block * capacity
        pick = jnp.where(row == slot, gate, 0.0).astype(BF16)
        outs[peers + block][...] = dot(pick, grad_ref[...], 1, 0).astype(BF16)


def unpack_kernel(capacity, width, peers, slot_ref, *refs):
    blocks, (feat_ref, gate_ref) = refs[:peers], refs[-2:]
    slot = slot_ref[...]
    count = slot.shape[1]
    total = None
    for block, ref in enumerate(blocks):
        row = lax.broadcasted_iota(jnp.int32, (capacity, count), 0) + block * capacity
        pick = jnp.where(row == slot, 1.0, 0.0).astype(BF16)
        part = dot(pick, ref[...], 0, 0)
        total = part if total is None else total + part
    feat_ref[...] = total[:, :width].astype(BF16)
    gate_ref[...] = total[:, width:]


def call(body, inputs, out_shape, name, after=()):
    return pl.pallas_call(
        body,
        in_specs=[WHOLE] * len(inputs) + [LATER] * len(after),
        out_specs=[WHOLE] * len(out_shape),
        out_shape=[jax.ShapeDtypeStruct(*s) for s in out_shape],
        compiler_params=params(),
        name=name,
    )(*inputs, *after)


def hidden_kernel(peers, tiles, *refs):
    blocks, up_ref = refs[:peers], refs[peers]
    flip_feat_ref, hidden_ref, flip_hidden_ref, slope_ref = refs[-4:]
    feat = jnp.concatenate([ref[...] for ref in blocks], axis=0)
    flip_feat_ref[...] = feat.T
    tile = up_ref.shape[2] // tiles
    for i in range(tiles):
        part = slice(i * tile, (i + 1) * tile)
        pre_act = dot(feat, up_ref[0, :, part], 1, 0)
        cdf = 0.5 * (1.0 + lax.erf(pre_act * SQRT_HALF))
        hidden = (pre_act * cdf).astype(BF16)
        hidden_ref[:, part] = hidden
        flip_hidden_ref[part, :] = hidden.T
        slope = cdf + pre_act * jnp.exp(-0.5 * pre_act * pre_act) * INV_ROOT_TAU
        slope_ref[:, part] = slope.astype(BF16)


def hidden_call(blocks, up_weight, after=()):
    _, width, inner = up_weight.shape
    rows = len(blocks) * blocks[0].shape[0]
    return call(
        functools.partial(hidden_kernel, len(blocks), 8),
        [*blocks, up_weight],
        [
            ((width, rows), BF16),
            ((rows, inner), BF16),
            ((inner, rows), BF16),
            ((rows, inner), BF16),
        ],
        "hidden",
        after,
    )


def pre_grad_kernel(peers, tiles, *refs):
    blocks = refs[:peers]
    down_ref, hidden_ref, slope_ref = refs[peers : peers + 3]
    pre_ref, sum_ref = refs[-2:]
    scaled = jnp.concatenate([ref[...] for ref in blocks], axis=0)
    tile = down_ref.shape[1] // tiles
    total = 0.0
    for i in range(tiles):
        part = slice(i * tile, (i + 1) * tile)
        hidden_grad = dot(scaled, down_ref[0, part, :], 1, 1)
        pre_ref[:, part] = (hidden_grad * slope_ref[:, part].astype(F32)).astype(BF16)
        product = hidden_grad * hidden_ref[:, part].astype(F32)
        for j in range(tile // LANES):
            total += product[:, j * LANES : (j + 1) * LANES]
    sum_ref[...] = jnp.broadcast_to(jnp.sum(total, axis=1, keepdims=True), sum_ref.shape)


def pre_grad_call(blocks, down_weight, hidden, slope, after=()):
    _, inner, width = down_weight.shape
    rows = len(blocks) * blocks[0].shape[0]
    return call(
        functools.partial(pre_grad_kernel, len(blocks), 8),
        [*blocks, down_weight, hidden, slope],
        [((rows, inner), BF16), ((rows, LANES), F32)],
        "pre_grad",
        after,
    )


def feat_grad_kernel(block, pre_ref, up_ref, sum_ref, *refs):
    out = refs[-1]
    capacity = out.shape[0]
    part = slice(block * capacity, (block + 1) * capacity)
    width = up_ref.shape[1]
    out[:, :width] = dot(pre_ref[part, :], up_ref[0], 1, 1).astype(BF16)
    total = sum_ref[part, :]
    high = total.astype(BF16).astype(F32)
    lane = lax.broadcasted_iota(jnp.int32, total.shape, 1)
    out[:, width:] = jnp.where(lane == 0, high, total - high).astype(BF16)


def feat_grad_call(pre_grad, up_weight, sums, block, capacity, after=()):
    shape = (capacity, up_weight.shape[1] + LANES)
    return call(
        functools.partial(feat_grad_kernel, block),
        [pre_grad, up_weight, sums],
        [(shape, BF16)],
        "feat_grad",
        after,
    )[0]


def ring_index(position, count):
    half = count // 2
    return jnp.where(position < half, 2 * position, 2 * (count - 1 - position) + 1)


def ring_position(index, count):
    return jnp.where(index % 2 == 0, index // 2, count - 1 - index // 2)


def ring_pairs(count):
    half = count // 2
    ring = [2 * p if p < half else 2 * (count - 1 - p) + 1 for p in range(count)]
    return [(ring[p], ring[(p + 1) % count]) for p in range(count)]


def step_kernel(parts, arrivals, step, count, order_ref, *refs):
    groups = len(parts)
    lefts, refs = refs[:groups], refs[groups:]
    last = step == count
    if last:
        out, held, sems = refs[-3:]
    else:
        outs = refs[-2:]
    half = refs[0].shape[1] // 2
    rows = lefts[0].shape[0] // count
    totals = [ref[...].astype(F32) for ref in refs[sum(parts) : sum(parts) + arrivals]] or [0.0] * 2
    for left, blocks in zip(lefts, parts):
        right = [ref[...] for ref in refs[:blocks]]
        right = right[0] if blocks == 1 else jnp.concatenate(right, axis=0)
        refs = refs[blocks:]
        for way in range(2):
            start = pl.multiple_of(order_ref[way, step - 1] * rows, rows)
            totals[way] += dot(
                left[pl.ds(start, rows), :], right[:, way * half : (way + 1) * half], 1, 0
            )
    copies = []
    for way in range(2):
        if last:
            held[way] = totals[way] * (1.0 / count)
            target = out.at[0, :, way * half : (way + 1) * half]
            copies.append(pltpu.make_async_copy(held.at[way], target, sems.at[way]))
            copies[-1].start()
        else:
            outs[way][...] = totals[way].astype(BF16)
    for copy in copies:
        copy.wait()


def ring_step(name, order, step, count, lefts, rights, arrived, after=()):
    rows = lefts[0].shape[0] // count
    width = rights[0][0].shape[1]
    if step == count:
        out_specs = [pl.BlockSpec(memory_space=pltpu.HBM)]
        out_shape = [pltpu.HBM((1, rows, width), F32)]
        scratch = [pltpu.VMEM((2, rows, width // 2), F32), pltpu.SemaphoreType.DMA((2,))]
    else:
        out_specs = [WHOLE] * 2
        out_shape = [jax.ShapeDtypeStruct((rows, width // 2), BF16)] * 2
        scratch = []
    blocks = [block for group in rights for block in group]
    inputs = [*lefts, *blocks, *arrived]
    return pl.pallas_call(
        functools.partial(
            step_kernel, [len(group) for group in rights], len(arrived), step, count
        ),
        in_specs=[pl.BlockSpec(memory_space=pltpu.SMEM)]
        + [WHOLE] * len(inputs)
        + [LATER] * len(after),
        out_specs=out_specs,
        out_shape=out_shape,
        scratch_shapes=scratch,
        compiler_params=params(),
        name=name,
    )(order, *inputs, *after)


def per_device(tokens, out_grad, gate_prob, expert_id, up_weight, down_weight):
    count, width = tokens.shape
    inner = up_weight.shape[2]
    peers = lax.axis_size("expert")
    experts = peers * up_weight.shape[0]
    capacity = 2 * count // experts
    ring = lax.axis_size("dp")
    me = lax.axis_index("expert")
    sources = [[(i, i ^ k) for i in range(peers)] for k in range(peers)]
    forward = ring_pairs(ring)
    backward = [(b, a) for a, b in forward]
    place = ring_position(lax.axis_index("dp"), ring)
    steps = jnp.arange(1, ring + 1, dtype=jnp.int32)
    order = ring_index(
        jnp.stack([(place - steps) % ring, (place + steps) % ring]), ring
    ).astype(jnp.int32)

    def exchange(outs, reach):
        return {k: lax.ppermute(outs[k], "expert", sources[k]) for k in reach}

    near, far = range(1, peers // 2), range(peers // 2, peers)
    hbm = pl.BlockSpec(memory_space=pltpu.HBM)
    slot, *packed = pl.pallas_call(
        functools.partial(pack_kernel, experts, capacity),
        in_specs=[pl.BlockSpec(memory_space=pltpu.SMEM)] + [hbm] * 4,
        out_specs=[WHOLE] * (1 + 2 * peers),
        out_shape=[jax.ShapeDtypeStruct((1, count), jnp.int32)]
        + [jax.ShapeDtypeStruct((capacity, width), BF16)] * (2 * peers),
        scratch_shapes=[
            pltpu.VMEM((count,), jnp.int32),
            pltpu.VMEM((count, width), BF16),
            pltpu.VMEM((count,), BF16),
            pltpu.VMEM((count, width), BF16),
            pltpu.SemaphoreType.DMA((4,)),
        ],
        compiler_params=params(),
        name="pack",
    )(me.reshape(1), *(in_hbm(a) for a in (expert_id, tokens, gate_prob, out_grad)))
    feat_out, grad_out = packed[:peers], packed[peers:]
    feat_in = {0: feat_out[0], **exchange(feat_out, far), **exchange(feat_out, near)}
    grad_in = {0: grad_out[0], **exchange(grad_out, far), **exchange(grad_out, near)}

    groups = [[0, *near], [*far]]
    feats = [[feat_in[k] for k in group] for group in groups]
    scaleds = [[grad_in[k] for k in group] for group in groups]
    near_hidden = hidden_call(feats[0], up_weight)
    near_pre = pre_grad_call(scaleds[0], down_weight, near_hidden[1], near_hidden[3])
    far_hidden = hidden_call(feats[1], up_weight, [near_pre[1]])
    flip_feats = [near_hidden[0], far_hidden[0]]
    flip_hiddens = [near_hidden[2], far_hidden[2]]

    def send(pair):
        return [lax.ppermute(pair[0], "dp", forward), lax.ppermute(pair[1], "dp", backward)]

    turn = 1 if ring < 8 else 2
    span = min(4, ring - turn)
    returns = [*far, *near, 0]
    feat_back = {}
    down_in, up_in, after, landed = [], [], [], []
    for step in range(1, ring + 1):
        down = ring_step("down_step", order, step, ring, flip_hiddens, scaleds, down_in, after)
        if step < ring:
            down_in = send(down)
            after = [down[0]]
        else:
            after = []
        if step == 1:
            far_pre = pre_grad_call(scaleds[1], down_weight, far_hidden[1], far_hidden[3], after)
            pre_grads = [[near_pre[0]], [far_pre[0]]]
            after = [far_pre[1]]
        up = ring_step("up_step", order, step, ring, flip_feats, pre_grads, up_in, after)
        if step < ring:
            up_in = send(up)
            after = [up[0]]
        after = after + landed
        landed = []
        first = (step - turn) * len(returns) // span
        stop = (step - turn + 1) * len(returns) // span
        for k in returns[max(first, 0) : max(stop, 0)]:
            group = int(k in far)
            block = feat_grad_call(
                pre_grads[group][0],
                up_weight,
                (near_pre, far_pre)[group][1],
                groups[group].index(k),
                capacity,
                after,
            )
            after = [block]
            feat_back[k] = lax.ppermute(block, "expert", sources[k]) if k else block
            landed.append(feat_back[k])
        if step == ring - 1:
            tokens_grad, gate_sums = pl.pallas_call(
                functools.partial(unpack_kernel, capacity, width, peers),
                in_specs=[WHOLE] * (1 + peers) + [LATER] * len(after),
                out_specs=[WHOLE] * 2,
                out_shape=[
                    jax.ShapeDtypeStruct((count, width), BF16),
                    jax.ShapeDtypeStruct((count, LANES), F32),
                ],
                compiler_params=params(),
                name="unpack",
            )(slot, *(feat_back[k] for k in range(peers)), *after)
            after = [gate_sums]
    gate_result = ((gate_sums[:, 0] + gate_sums[:, 1]) / gate_prob.astype(F32)).astype(BF16)
    return (tokens_grad, gate_result, up[0], down[0])


def solution(mesh):
    return jax.shard_map(
        per_device,
        mesh=mesh,
        in_specs=(
            P(("dp", "expert"), None),
            P(("dp", "expert"), None),
            P(("dp", "expert")),
            P(("dp", "expert")),
            P("expert", None, None),
            P("expert", None, None),
        ),
        out_specs=(
            P(("dp", "expert"), None),
            P(("dp", "expert")),
            P("expert", "dp", None),
            P("expert", "dp", None),
        ),
        check_vma=False,
    )
```

```python
import functools

import jax
import jax.numpy as jnp
from jax import lax
from jax.experimental import pallas as pl
from jax.experimental.pallas import tpu as pltpu
from jax.sharding import PartitionSpec as P

SQRT_HALF = 0.7071067811865476
INV_ROOT_TAU = 0.3989422804014327
LANES = 128
VMEM_LIMIT = 16 * 1024 * 1024
F32 = jnp.float32
BF16 = jnp.bfloat16
WHOLE = pl.BlockSpec(memory_space=pltpu.VMEM)
LATER = pl.BlockSpec(memory_space=pl.ANY)


def in_hbm(array):
    return pltpu.with_memory_space_constraint(array, pltpu.HBM)


def params(*semantics):
    return pltpu.CompilerParams(
        vmem_limit_bytes=VMEM_LIMIT, dimension_semantics=semantics or None
    )


def dot(left, right, left_dim, right_dim):
    return lax.dot_general(
        left, right, (((left_dim,), (right_dim,)), ((), ())), preferred_element_type=F32
    )


def slot_row(id_row, experts, capacity, me):
    count = id_row.shape[1]
    expert = lax.broadcasted_iota(jnp.int32, (max(experts, 8), count), 0)
    chosen = expert == id_row
    earlier = lax.broadcasted_iota(jnp.int32, (count, count), 0) < lax.broadcasted_iota(
        jnp.int32, (count, count), 1
    )
    before = dot(
        jnp.where(chosen, 1.0, 0.0).astype(BF16), jnp.where(earlier, 1.0, 0.0).astype(BF16), 1, 0
    )
    position = jnp.sum(jnp.where(chosen, before, 0.0), axis=0, keepdims=True).astype(jnp.int32)
    return (id_row ^ me) * capacity + position


def pick_rows(slot, block, capacity, value):
    row = lax.broadcasted_iota(jnp.int32, (capacity, slot.shape[1]), 0) + block * capacity
    return jnp.where(row == slot, value, 0.0).astype(BF16)


def pack_kernel(experts, capacity, near, *refs):
    sources, refs = refs[:4], refs[4:]
    slot_ref, outs = refs[0], refs[1:-5]
    held, sems = refs[-5:-1], refs[-1]
    copies = [
        pltpu.make_async_copy(source, target, sems.at[i])
        for i, (source, target) in enumerate(zip(sources, held))
    ]
    for copy in copies:
        copy.start()
    id_ref, gate_ref, grad_ref, tokens_ref = held
    copies[0].wait()
    count = id_ref.shape[0]
    slot = slot_row(id_ref[...].reshape(1, count), experts, capacity, lax.axis_index("expert"))
    slot_ref[...] = slot
    for copy in copies[1:]:
        copy.wait()
    gate = gate_ref[...].astype(F32).reshape(1, count)
    for block, out in enumerate(outs[near:]):
        out[...] = dot(pick_rows(slot, block, capacity, gate), grad_ref[...], 1, 0).astype(BF16)
    for block, out in enumerate(outs[:near]):
        out[...] = dot(pick_rows(slot, block, capacity, 1.0), tokens_ref[...], 1, 0).astype(BF16)


def repack_kernel(experts, capacity, id_ref, tokens_ref, _, *outs):
    slot = slot_row(id_ref[...], experts, capacity, lax.axis_index("expert"))
    for block, out in enumerate(outs):
        out[...] = dot(pick_rows(slot, block, capacity, 1.0), tokens_ref[...], 1, 0).astype(BF16)


def unpack_kernel(capacity, width, peers, slot_ref, *refs):
    blocks, (feat_ref, gate_ref) = refs[:peers], refs[-2:]
    slot = slot_ref[...]
    count = slot.shape[1]
    total = None
    for block, ref in enumerate(blocks):
        row = lax.broadcasted_iota(jnp.int32, (capacity, count), 0) + block * capacity
        pick = jnp.where(row == slot, 1.0, 0.0).astype(BF16)
        part = dot(pick, ref[...], 0, 0)
        total = part if total is None else total + part
    feat_ref[...] = total[:, :width].astype(BF16)
    gate_ref[...] = total[:, width:]


def call(body, inputs, out_shape, name, after=()):
    return pl.pallas_call(
        body,
        in_specs=[WHOLE] * len(inputs) + [LATER] * len(after),
        out_specs=[WHOLE] * len(out_shape),
        out_shape=[jax.ShapeDtypeStruct(*s) for s in out_shape],
        compiler_params=params(),
        name=name,
    )(*inputs, *after)


def hidden_kernel(peers, tiles, *refs):
    blocks, up_ref = refs[:peers], refs[peers]
    flip_feat_ref, hidden_ref, flip_hidden_ref, slope_ref = refs[-4:]
    feat = jnp.concatenate([ref[...] for ref in blocks], axis=0)
    flip_feat_ref[...] = feat.T
    tile = up_ref.shape[2] // tiles
    for i in range(tiles):
        part = slice(i * tile, (i + 1) * tile)
        pre_act = dot(feat, up_ref[0, :, part], 1, 0)
        cdf = 0.5 * (1.0 + lax.erf(pre_act * SQRT_HALF))
        hidden = (pre_act * cdf).astype(BF16)
        hidden_ref[:, part] = hidden
        flip_hidden_ref[part, :] = hidden.T
        slope = cdf + pre_act * jnp.exp(-0.5 * pre_act * pre_act) * INV_ROOT_TAU
        slope_ref[:, part] = slope.astype(BF16)


def hidden_call(blocks, up_weight, after=()):
    _, width, inner = up_weight.shape
    rows = len(blocks) * blocks[0].shape[0]
    return call(
        functools.partial(hidden_kernel, len(blocks), 8),
        [*blocks, up_weight],
        [
            ((width, rows), BF16),
            ((rows, inner), BF16),
            ((inner, rows), BF16),
            ((rows, inner), BF16),
        ],
        "hidden",
        after,
    )


def pre_grad_kernel(peers, tiles, *refs):
    blocks = refs[:peers]
    down_ref, hidden_ref, slope_ref = refs[peers : peers + 3]
    pre_ref, sum_ref = refs[-2:]
    scaled = jnp.concatenate([ref[...] for ref in blocks], axis=0)
    tile = down_ref.shape[1] // tiles
    total = 0.0
    for i in range(tiles):
        part = slice(i * tile, (i + 1) * tile)
        hidden_grad = dot(scaled, down_ref[0, part, :], 1, 1)
        pre_ref[:, part] = (hidden_grad * slope_ref[:, part].astype(F32)).astype(BF16)
        product = hidden_grad * hidden_ref[:, part].astype(F32)
        for j in range(tile // LANES):
            total += product[:, j * LANES : (j + 1) * LANES]
    sum_ref[...] = jnp.broadcast_to(jnp.sum(total, axis=1, keepdims=True), sum_ref.shape)


def pre_grad_call(blocks, down_weight, hidden, slope, after=()):
    _, inner, width = down_weight.shape
    rows = len(blocks) * blocks[0].shape[0]
    return call(
        functools.partial(pre_grad_kernel, len(blocks), 8),
        [*blocks, down_weight, hidden, slope],
        [((rows, inner), BF16), ((rows, LANES), F32)],
        "pre_grad",
        after,
    )


def feat_grad_kernel(block, pre_ref, up_ref, sum_ref, *refs):
    out = refs[-1]
    capacity = out.shape[0]
    part = slice(block * capacity, (block + 1) * capacity)
    width = up_ref.shape[1]
    out[:, :width] = dot(pre_ref[part, :], up_ref[0], 1, 1).astype(BF16)
    total = sum_ref[part, :]
    high = total.astype(BF16).astype(F32)
    lane = lax.broadcasted_iota(jnp.int32, total.shape, 1)
    out[:, width:] = jnp.where(lane == 0, high, total - high).astype(BF16)


def feat_grad_call(pre_grad, up_weight, sums, block, capacity, after=()):
    shape = (capacity, up_weight.shape[1] + LANES)
    return call(
        functools.partial(feat_grad_kernel, block),
        [pre_grad, up_weight, sums],
        [(shape, BF16)],
        "feat_grad",
        after,
    )[0]


def ring_chunk(step, count):
    index = lax.axis_index("dp")
    half = lax.div(index, 2)
    place = jnp.where(lax.rem(index, 2) == 0, half, count - 1 - half)
    chunks = []
    for move in (count - step, step):
        position = lax.rem(place + move, count)
        mirror = 2 * (count - 1 - position) + 1
        chunks.append(jnp.where(position < count // 2, 2 * position, mirror))
    return chunks


def ring_pairs(count):
    half = count // 2
    ring = [2 * p if p < half else 2 * (count - 1 - p) + 1 for p in range(count)]
    return [(ring[p], ring[(p + 1) % count]) for p in range(count)]


def step_kernel(parts, arrivals, step, count, last, *refs):
    groups = len(parts)
    lefts, refs = refs[:groups], refs[groups:]
    rights, refs = refs[: sum(parts)], refs[sum(parts) :]
    totals = [0.0, 0.0]
    chunks = ring_chunk(step, count) if groups else None
    for i, ref in enumerate(refs[:arrivals]):
        totals[i % 2] += ref[...].astype(F32)
    for left, blocks in zip(lefts, parts):
        right = [ref[...] for ref in rights[:blocks]]
        right = right[0] if blocks == 1 else jnp.concatenate(right, axis=0)
        rights = rights[blocks:]
        half = right.shape[1] // 2
        rows = left.shape[0] // count
        for way in range(2):
            start = pl.multiple_of(chunks[way] * rows, rows)
            totals[way] += dot(
                left[pl.ds(start, rows), :], right[:, way * half : (way + 1) * half], 1, 0
            )
    if not last:
        for way, out in enumerate(refs[-2:]):
            out[...] = totals[way].astype(out.dtype)
        return
    out, held, sems = refs[-3:]
    half = held.shape[2]
    copies = []
    for way in range(2):
        held[way] = totals[way] * (1.0 / count)
        target = out.at[0, :, way * half : (way + 1) * half]
        copies.append(pltpu.make_async_copy(held.at[way], target, sems.at[way]))
        copies[-1].start()
    for copy in copies:
        copy.wait()


def ring_step(name, step, count, shape, lefts, rights, arrived, after=(), dtype=BF16):
    rows, half = shape
    last = dtype is None
    if last:
        out_specs = [pl.BlockSpec(memory_space=pltpu.HBM)]
        out_shape = [pltpu.HBM((1, rows, 2 * half), F32)]
        scratch = [pltpu.VMEM((2, rows, half), F32), pltpu.SemaphoreType.DMA((2,))]
    else:
        out_specs = [WHOLE] * 2
        out_shape = [jax.ShapeDtypeStruct(shape, dtype)] * 2
        scratch = []
    blocks = [block for group in rights for block in group]
    inputs = [*lefts, *blocks, *arrived]
    return pl.pallas_call(
        functools.partial(
            step_kernel, [len(group) for group in rights], len(arrived), step, count, last
        ),
        in_specs=[WHOLE] * len(inputs) + [LATER] * len(after),
        out_specs=out_specs,
        out_shape=out_shape,
        scratch_shapes=scratch,
        compiler_params=params(),
        name=name,
    )(*inputs, *after)


def per_device(tokens, out_grad, gate_prob, expert_id, up_weight, down_weight):
    count, width = tokens.shape
    inner = up_weight.shape[2]
    peers = lax.axis_size("expert")
    experts = peers * up_weight.shape[0]
    capacity = 2 * count // experts
    ring = lax.axis_size("dp")
    sources = [[(i, i ^ k) for i in range(peers)] for k in range(peers)]
    forward = ring_pairs(ring)
    backward = [(b, a) for a, b in forward]

    def exchange(outs, reach):
        return {k: lax.ppermute(outs[k], "expert", sources[k]) for k in reach}

    near, far = range(1, peers // 2), range(peers // 2, peers)
    hbm = pl.BlockSpec(memory_space=pltpu.HBM)
    across = [(i, i ^ peers // 2) for i in range(peers)]
    tokens_across = lax.ppermute(tokens, "expert", across)
    id_across = lax.ppermute(expert_id.reshape(1, count), "expert", across)

    block_shape = jax.ShapeDtypeStruct((capacity, width), BF16)
    slot, *packed = pl.pallas_call(
        functools.partial(pack_kernel, experts, capacity, peers // 2),
        in_specs=[hbm] * 4,
        out_specs=[WHOLE] * (1 + peers // 2 + peers),
        out_shape=[jax.ShapeDtypeStruct((1, count), jnp.int32)]
        + [block_shape] * (peers // 2 + peers),
        scratch_shapes=[
            pltpu.VMEM((count,), jnp.int32),
            pltpu.VMEM((count,), BF16),
            pltpu.VMEM((count, width), BF16),
            pltpu.VMEM((count, width), BF16),
            pltpu.SemaphoreType.DMA((4,)),
        ],
        compiler_params=params(),
        name="pack",
    )(*(in_hbm(a) for a in (expert_id, gate_prob, out_grad, tokens)))
    feat_out, grad_out = packed[: peers // 2], packed[peers // 2 :]
    grad_in = {0: grad_out[0], **exchange(grad_out, far), **exchange(grad_out, near)}
    feat_in = {0: feat_out[0], **exchange(feat_out, near)}
    groups = [[0, *near], [peers // 2], [*far][1:]]
    groups = [group for group in groups if group]
    scaleds = [[grad_in[k] for k in group] for group in groups]
    hiddens, pre_grads, sums = [], [], []

    def add_hidden(blocks, after=()):
        hiddens.append(hidden_call(blocks, up_weight, after))
        return [hiddens[-1][1]]

    def add_pre_grad(after=()):
        group = len(pre_grads)
        _, hidden, _, slope = hiddens[group]
        pre, total = pre_grad_call(scaleds[group], down_weight, hidden, slope, after)
        pre_grads.append([pre])
        sums.append(total)
        return [total]

    add_hidden([feat_in[k] for k in groups[0]])
    after = add_pre_grad()
    across_out = pl.pallas_call(
        functools.partial(repack_kernel, experts, capacity),
        in_specs=[WHOLE, WHOLE, LATER],
        out_specs=[WHOLE] * (peers // 2),
        out_shape=[block_shape] * (peers // 2),
        compiler_params=params(),
        name="repack",
    )(id_across, tokens_across, *after)
    across_in = exchange(across_out, near)
    after = add_hidden(across_out[:1])
    if len(groups) > 2:
        after = add_pre_grad(after)
        after = add_hidden([across_in[k] for k in near], after)
    flip_feats = [part[0] for part in hiddens]
    flip_hiddens = [part[2] for part in hiddens]
    down_shape = (inner // ring, width // 2)
    up_shape = (width // ring, inner // 2)
    down_in = ring_step(
        "down_early",
        1,
        ring,
        down_shape,
        flip_hiddens[:-1],
        scaleds[:-1],
        [],
        after,
        F32,
    )

    def send(pair):
        return [lax.ppermute(pair[0], "dp", forward), lax.ppermute(pair[1], "dp", backward)]

    turn = 1 if ring < 8 else 2
    span = min(4, ring - turn)
    returns = [*far, *near, 0]
    feat_back = {}
    up_in, after, landed = [], [], []
    for step in range(1, ring):
        late = slice(-1, None) if step == 1 else slice(None)
        down = ring_step(
            "down_step",
                step,
            ring,
            down_shape,
            flip_hiddens[late],
            scaleds[late],
            down_in,
            after,
        )
        down_in = send(down)
        after = [*down]
        if step == 1:
            after = add_pre_grad(after)
        up = ring_step(
            "up_step", step, ring, up_shape, flip_feats, pre_grads, up_in, after
        )
        up_in = send(up)
        after = [*up] + landed
        landed = []
        first = (step - turn) * len(returns) // span
        stop = (step - turn + 1) * len(returns) // span
        for k in returns[max(first, 0) : max(stop, 0)]:
            group = [k in members for members in groups].index(True)
            block = feat_grad_call(
                pre_grads[group][0],
                up_weight,
                sums[group],
                groups[group].index(k),
                capacity,
                after,
            )
            after = [block]
            feat_back[k] = lax.ppermute(block, "expert", sources[k]) if k else block
            landed.append(feat_back[k])
        if step == max(ring - 2, 1):
            down_last = ring_step(
                "down_own",
                        ring,
                ring,
                down_shape,
                flip_hiddens,
                scaleds,
                [],
                after,
                F32,
            )
            up_last = ring_step(
                "up_own",
                        ring,
                ring,
                up_shape,
                flip_feats,
                pre_grads,
                [],
                down_last[:1],
                F32,
            )
            after = up_last[:1]
    down = ring_step(
        "down_last", ring, ring, down_shape, [], [], [*down_in, *down_last], [], None
    )
    after_down = [in_hbm(down[0])]
    up = ring_step(
        "up_last", ring, ring, up_shape, [], [], [*up_in, *up_last], after_down, None
    )
    tokens_grad, gate_sums = pl.pallas_call(
        functools.partial(unpack_kernel, capacity, width, peers),
        in_specs=[WHOLE] * (1 + peers) + [LATER] * len(after),
        out_specs=[WHOLE] * 2,
        out_shape=[
            jax.ShapeDtypeStruct((count, width), BF16),
            jax.ShapeDtypeStruct((count, LANES), F32),
        ],
        compiler_params=params(),
        name="unpack",
    )(slot, *(feat_back[k] for k in range(peers)), *after)
    gate_result = ((gate_sums[:, 0] + gate_sums[:, 1]) / gate_prob.astype(F32)).astype(BF16)
    return (tokens_grad, gate_result, up[0], down[0])


def solution(mesh):
    return jax.shard_map(
        per_device,
        mesh=mesh,
        in_specs=(
            P(("dp", "expert"), None),
            P(("dp", "expert"), None),
            P(("dp", "expert")),
            P(("dp", "expert")),
            P("expert", None, None),
            P("expert", None, None),
        ),
        out_specs=(
            P(("dp", "expert"), None),
            P(("dp", "expert")),
            P("expert", "dp", None),
            P("expert", "dp", None),
        ),
        check_vma=False,
    )
```

```python
import functools

import jax
import jax.numpy as jnp
from jax import lax
from jax.experimental import pallas as pl
from jax.experimental.pallas import tpu as pltpu
from jax.sharding import PartitionSpec as P

SQRT_HALF = 0.7071067811865476
INV_ROOT_TAU = 0.3989422804014327
LANES = 128
VMEM_LIMIT = 16 * 1024 * 1024
F32 = jnp.float32
BF16 = jnp.bfloat16
WHOLE = pl.BlockSpec(memory_space=pltpu.VMEM)
LATER = pl.BlockSpec(memory_space=pl.ANY)


def in_hbm(array):
    return pltpu.with_memory_space_constraint(array, pltpu.HBM)


def params(*semantics):
    return pltpu.CompilerParams(
        vmem_limit_bytes=VMEM_LIMIT, dimension_semantics=semantics or None
    )


def dot(left, right, left_dim, right_dim):
    return lax.dot_general(
        left, right, (((left_dim,), (right_dim,)), ((), ())), preferred_element_type=F32
    )


def slot_row(id_row, experts, capacity, me):
    count = id_row.shape[1]
    expert = lax.broadcasted_iota(jnp.int32, (max(experts, 8), count), 0)
    chosen = expert == id_row
    earlier = lax.broadcasted_iota(jnp.int32, (count, count), 0) < lax.broadcasted_iota(
        jnp.int32, (count, count), 1
    )
    before = dot(
        jnp.where(chosen, 1.0, 0.0).astype(BF16), jnp.where(earlier, 1.0, 0.0).astype(BF16), 1, 0
    )
    position = jnp.sum(jnp.where(chosen, before, 0.0), axis=0, keepdims=True).astype(jnp.int32)
    return (id_row ^ me) * capacity + position


def pick_rows(slot, block, capacity, value):
    row = lax.broadcasted_iota(jnp.int32, (capacity, slot.shape[1]), 0) + block * capacity
    return jnp.where(row == slot, value, 0.0).astype(BF16)


def pack_kernel(experts, capacity, near, *refs):
    sources, refs = refs[:4], refs[4:]
    slot_ref, outs = refs[0], refs[1:-5]
    held, sems = refs[-5:-1], refs[-1]
    copies = [
        pltpu.make_async_copy(source, target, sems.at[i])
        for i, (source, target) in enumerate(zip(sources, held))
    ]
    for copy in copies:
        copy.start()
    id_ref, gate_ref, grad_ref, tokens_ref = held
    copies[0].wait()
    count = id_ref.shape[0]
    slot = slot_row(id_ref[...].reshape(1, count), experts, capacity, lax.axis_index("expert"))
    slot_ref[...] = slot
    for copy in copies[1:]:
        copy.wait()
    gate = gate_ref[...].astype(F32).reshape(1, count)
    for block, out in enumerate(outs[near:]):
        out[...] = dot(pick_rows(slot, block, capacity, gate), grad_ref[...], 1, 0).astype(BF16)
    for block, out in enumerate(outs[:near]):
        out[...] = dot(pick_rows(slot, block, capacity, 1.0), tokens_ref[...], 1, 0).astype(BF16)


def repack_kernel(experts, capacity, id_ref, tokens_ref, _, *outs):
    slot = slot_row(id_ref[...], experts, capacity, lax.axis_index("expert"))
    for block, out in enumerate(outs):
        out[...] = dot(pick_rows(slot, block, capacity, 1.0), tokens_ref[...], 1, 0).astype(BF16)


def unpack_kernel(capacity, width, peers, slot_ref, *refs):
    blocks, (feat_ref, gate_ref) = refs[:peers], refs[-2:]
    slot = slot_ref[...]
    count = slot.shape[1]
    total = None
    for block, ref in enumerate(blocks):
        row = lax.broadcasted_iota(jnp.int32, (capacity, count), 0) + block * capacity
        pick = jnp.where(row == slot, 1.0, 0.0).astype(BF16)
        part = dot(pick, ref[...], 0, 0)
        total = part if total is None else total + part
    feat_ref[...] = total[:, :width].astype(BF16)
    gate_ref[...] = total[:, width:]


def call(body, inputs, out_shape, name, after=()):
    return pl.pallas_call(
        body,
        in_specs=[WHOLE] * len(inputs) + [LATER] * len(after),
        out_specs=[WHOLE] * len(out_shape),
        out_shape=[jax.ShapeDtypeStruct(*s) for s in out_shape],
        compiler_params=params(),
        name=name,
    )(*inputs, *after)


def hidden_kernel(peers, tiles, *refs):
    blocks, up_ref = refs[:peers], refs[peers]
    flip_feat_ref, hidden_ref, flip_hidden_ref, slope_ref = refs[-4:]
    feat = jnp.concatenate([ref[...] for ref in blocks], axis=0)
    flip_feat_ref[...] = feat.T
    tile = up_ref.shape[2] // tiles
    for i in range(tiles):
        part = slice(i * tile, (i + 1) * tile)
        pre_act = dot(feat, up_ref[0, :, part], 1, 0)
        cdf = 0.5 * (1.0 + lax.erf(pre_act * SQRT_HALF))
        hidden = (pre_act * cdf).astype(BF16)
        hidden_ref[:, part] = hidden
        flip_hidden_ref[part, :] = hidden.T
        slope = cdf + pre_act * jnp.exp(-0.5 * pre_act * pre_act) * INV_ROOT_TAU
        slope_ref[:, part] = slope.astype(BF16)


def hidden_call(blocks, up_weight, after=()):
    _, width, inner = up_weight.shape
    rows = len(blocks) * blocks[0].shape[0]
    return call(
        functools.partial(hidden_kernel, len(blocks), 8),
        [*blocks, up_weight],
        [
            ((width, rows), BF16),
            ((rows, inner), BF16),
            ((inner, rows), BF16),
            ((rows, inner), BF16),
        ],
        "hidden",
        after,
    )


def pre_grad_kernel(peers, tiles, *refs):
    blocks = refs[:peers]
    down_ref, hidden_ref, slope_ref = refs[peers : peers + 3]
    pre_ref, sum_ref = refs[-2:]
    scaled = jnp.concatenate([ref[...] for ref in blocks], axis=0)
    tile = down_ref.shape[1] // tiles
    total = 0.0
    for i in range(tiles):
        part = slice(i * tile, (i + 1) * tile)
        hidden_grad = dot(scaled, down_ref[0, part, :], 1, 1)
        pre_ref[:, part] = (hidden_grad * slope_ref[:, part].astype(F32)).astype(BF16)
        product = hidden_grad * hidden_ref[:, part].astype(F32)
        for j in range(tile // LANES):
            total += product[:, j * LANES : (j + 1) * LANES]
    sum_ref[...] = jnp.broadcast_to(jnp.sum(total, axis=1, keepdims=True), sum_ref.shape)


def pre_grad_call(blocks, down_weight, hidden, slope, after=()):
    _, inner, width = down_weight.shape
    rows = len(blocks) * blocks[0].shape[0]
    return call(
        functools.partial(pre_grad_kernel, len(blocks), 8),
        [*blocks, down_weight, hidden, slope],
        [((rows, inner), BF16), ((rows, LANES), F32)],
        "pre_grad",
        after,
    )


def feat_grad_kernel(block, pre_ref, up_ref, sum_ref, *refs):
    out = refs[-1]
    capacity = out.shape[0]
    part = slice(block * capacity, (block + 1) * capacity)
    width = up_ref.shape[1]
    out[:, :width] = dot(pre_ref[part, :], up_ref[0], 1, 1).astype(BF16)
    total = sum_ref[part, :]
    high = total.astype(BF16).astype(F32)
    lane = lax.broadcasted_iota(jnp.int32, total.shape, 1)
    out[:, width:] = jnp.where(lane == 0, high, total - high).astype(BF16)


def feat_grad_call(pre_grad, up_weight, sums, block, capacity, after=()):
    shape = (capacity, up_weight.shape[1] + LANES)
    return call(
        functools.partial(feat_grad_kernel, block),
        [pre_grad, up_weight, sums],
        [(shape, BF16)],
        "feat_grad",
        after,
    )[0]


def ring_chunk(offset, count):
    index = lax.axis_index("dp")
    half = lax.div(index, 2)
    place = jnp.where(lax.rem(index, 2) == 0, half, count - 1 - half)
    position = lax.rem(place + (offset + count), count)
    mirror = 2 * (count - 1 - position) + 1
    return jnp.where(position < count // 2, 2 * position, mirror)


def ring_targets(step, count):
    targets = []
    for way, sign in ((0, 1), (1, -1)):
        for side in range(2):
            offset = count // 2 - step + (side == way)
            if offset > 0:
                targets.append(((way, side), sign * offset))
    return targets


def ring_pairs(count):
    half = count // 2
    ring = [2 * p if p < half else 2 * (count - 1 - p) + 1 for p in range(count)]
    return [(ring[p], ring[(p + 1) % count]) for p in range(count)]


def step_kernel(parts, arrivals, targets, count, half, *refs):
    groups = len(parts)
    lefts, refs = refs[:groups], refs[groups:]
    rights, refs = refs[: sum(parts)], refs[sum(parts) :]
    totals = {key: 0.0 for key, _ in targets}
    for ref, (way, sides) in zip(refs, arrivals):
        for i, side in enumerate(sides):
            if (way, side) in totals:
                totals[way, side] += ref[:, i * half : (i + 1) * half].astype(F32)
    for left, blocks in zip(lefts, parts):
        rows = left.shape[0] // count
        for side in range(2):
            wanted = [(key, offset) for key, offset in targets if key[1] == side]
            if not wanted:
                continue
            right = [
                ref[...] if ref.shape[1] == half else ref[:, side * half : (side + 1) * half]
                for ref in rights[:blocks]
            ]
            right = right[0] if blocks == 1 else jnp.concatenate(right, axis=0)
            picked = []
            for _, offset in wanted:
                start = pl.multiple_of(ring_chunk(offset, count) * rows, rows)
                picked.append(left[pl.ds(start, rows), :])
            picked = picked[0] if len(picked) == 1 else jnp.concatenate(picked, axis=0)
            product = dot(picked, right, 1, 0)
            for i, (key, _) in enumerate(wanted):
                totals[key] += product[i * rows : (i + 1) * rows]
        rights = rights[blocks:]
    ways = sorted({way for way, _ in totals})
    for way, out in zip(ways, refs[-len(ways) :]):
        for i, key in enumerate(sorted(key for key in totals if key[0] == way)):
            out[:, i * half : (i + 1) * half] = totals[key].astype(out.dtype)


def ring_step(name, targets, count, shape, lefts, rights, arrived, after=(), dtype=BF16):
    rows, half = shape
    held = {}
    for way, side in sorted(key for key, _ in targets):
        held.setdefault(way, []).append(side)
    blocks = [block for group in rights for block in group]
    outs = call(
        functools.partial(
            step_kernel,
            [len(group) for group in rights],
            [(way, sides) for _, way, sides in arrived],
            targets,
            count,
            half,
        ),
        [*lefts, *blocks, *(array for array, _, _ in arrived)],
        [((rows, half * len(sides)), dtype) for sides in held.values()],
        name,
        after,
    )
    return [(out, way, tuple(sides)) for out, (way, sides) in zip(outs, held.items())]


def last_kernel(count, own_ref, *refs):
    arrived, (out, held, sems) = refs[:2], refs[-3:]
    half = held.shape[2]
    copies = []
    for side, ref in enumerate(arrived):
        part = slice(side * half, (side + 1) * half)
        held[side] = (own_ref[:, part] + ref[...].astype(F32)) * (1.0 / count)
        copies.append(pltpu.make_async_copy(held.at[side], out.at[0, :, part], sems.at[side]))
        copies[-1].start()
    for copy in copies:
        copy.wait()


def last_call(name, count, own, arrived, after):
    rows, width = own.shape
    return pl.pallas_call(
        functools.partial(last_kernel, count),
        in_specs=[WHOLE] * 3 + [LATER] * len(after),
        out_specs=pl.BlockSpec(memory_space=pltpu.HBM),
        out_shape=pltpu.HBM((1, rows, width), F32),
        scratch_shapes=[pltpu.VMEM((2, rows, width // 2), F32), pltpu.SemaphoreType.DMA((2,))],
        compiler_params=params(),
        name=name,
    )(own, *arrived, *after)


def per_device(tokens, out_grad, gate_prob, expert_id, up_weight, down_weight):
    count, width = tokens.shape
    inner = up_weight.shape[2]
    peers = lax.axis_size("expert")
    experts = peers * up_weight.shape[0]
    capacity = 2 * count // experts
    ring = lax.axis_size("dp")
    sources = [[(i, i ^ k) for i in range(peers)] for k in range(peers)]
    forward = ring_pairs(ring)
    backward = [(b, a) for a, b in forward]

    def exchange(outs, reach):
        return {k: lax.ppermute(outs[k], "expert", sources[k]) for k in reach}

    near, far = range(1, peers // 2), range(peers // 2, peers)
    hbm = pl.BlockSpec(memory_space=pltpu.HBM)
    across = [(i, i ^ peers // 2) for i in range(peers)]
    tokens_across = lax.ppermute(tokens, "expert", across)
    id_across = lax.ppermute(expert_id.reshape(1, count), "expert", across)

    block_shape = jax.ShapeDtypeStruct((capacity, width), BF16)
    slot, *packed = pl.pallas_call(
        functools.partial(pack_kernel, experts, capacity, peers // 2),
        in_specs=[hbm] * 4,
        out_specs=[WHOLE] * (1 + peers // 2 + peers),
        out_shape=[jax.ShapeDtypeStruct((1, count), jnp.int32)]
        + [block_shape] * (peers // 2 + peers),
        scratch_shapes=[
            pltpu.VMEM((count,), jnp.int32),
            pltpu.VMEM((count,), BF16),
            pltpu.VMEM((count, width), BF16),
            pltpu.VMEM((count, width), BF16),
            pltpu.SemaphoreType.DMA((4,)),
        ],
        compiler_params=params(),
        name="pack",
    )(*(in_hbm(a) for a in (expert_id, gate_prob, out_grad, tokens)))
    feat_out, grad_out = packed[: peers // 2], packed[peers // 2 :]
    grad_in = {0: grad_out[0], **exchange(grad_out, far), **exchange(grad_out, near)}
    feat_in = {0: feat_out[0], **exchange(feat_out, near)}
    groups = [[0, *near], [peers // 2], [*far][1:]]
    groups = [group for group in groups if group]
    scaleds = [[grad_in[k] for k in group] for group in groups]
    hiddens, pre_grads, sums = [], [], []

    def add_hidden(blocks, after=()):
        hiddens.append(hidden_call(blocks, up_weight, after))
        return [hiddens[-1][1]]

    def add_pre_grad(after=()):
        group = len(pre_grads)
        _, hidden, _, slope = hiddens[group]
        pre, total = pre_grad_call(scaleds[group], down_weight, hidden, slope, after)
        pre_grads.append([pre])
        sums.append(total)
        return [total]

    add_hidden([feat_in[k] for k in groups[0]])
    after = add_pre_grad()
    across_out = pl.pallas_call(
        functools.partial(repack_kernel, experts, capacity),
        in_specs=[WHOLE, WHOLE, LATER],
        out_specs=[WHOLE] * (peers // 2),
        out_shape=[block_shape] * (peers // 2),
        compiler_params=params(),
        name="repack",
    )(id_across, tokens_across, *after)
    across_in = exchange(across_out, near)
    after = add_hidden(across_out[:1])
    if len(groups) > 2:
        after = add_pre_grad(after)
        after = add_hidden([across_in[k] for k in near], after)
    flip_feats = [part[0] for part in hiddens]
    flip_hiddens = [part[2] for part in hiddens]
    down_shape = (inner // ring, width // 2)
    up_shape = (width // ring, inner // 2)
    early = ring_step(
        "down_early",
        ring_targets(1, ring),
        ring,
        down_shape,
        flip_hiddens[:-1],
        scaleds[:-1],
        [],
        after,
        F32,
    )
    after = [early[0][0]]

    def send(messages):
        ways = (forward, backward)
        return [(lax.ppermute(a, "dp", ways[way]), way, sides) for a, way, sides in messages]

    hops = ring // 2
    returns = [*far, *near, 0]
    spread = max(min(4, 2 * hops - 2), 1)
    feat_back, landed, slots = {}, [], []

    def give_back(after):
        slots.append(0)
        first = (len(slots) - 1) * len(returns) // spread
        stop = len(slots) * len(returns) // spread
        after = [*after, *landed]
        landed.clear()
        for k in returns[first:stop]:
            group = [k in members for members in groups].index(True)
            block = feat_grad_call(
                pre_grads[group][0],
                up_weight,
                sums[group],
                groups[group].index(k),
                capacity,
                after,
            )
            after = [block]
            feat_back[k] = lax.ppermute(block, "expert", sources[k]) if k else block
            landed.append(feat_back[k])
        return after

    def own(name, shape, lefts, rights, arrived, after):
        done = [
            (a, 0, tuple(None if side == way else side for side in sides))
            for a, way, sides in arrived
        ]
        targets = [((0, 0), 0), ((0, 1), 0)]
        return ring_step(name, targets, ring, shape, lefts, rights, done, after, F32)[0][0]

    down_in, up_in = [], []
    for step in range(1, hops + 1):
        targets = ring_targets(step, ring)
        if step == 1:
            messages = ring_step(
                "down_step",
                targets,
                ring,
                down_shape,
                flip_hiddens[-1:],
                scaleds[-1:],
                early,
                after,
            )
            down_in = send(messages)
            after = add_pre_grad([a for a, _, _ in messages])
        else:
            messages = ring_step(
                "down_step", targets, ring, down_shape, flip_hiddens, scaleds, down_in, after
            )
            after = [a for a, _, _ in messages]
            if step == hops:
                down_own = own(
                    "down_own", down_shape, flip_hiddens, scaleds, down_in, after
                )
                after = [down_own]
            else:
                after = give_back(after)
            down_in = send(messages)
        messages = ring_step(
            "up_step", targets, ring, up_shape, flip_feats, pre_grads, up_in, after
        )
        after = [a for a, _, _ in messages]
        if step == hops:
            up_own = own("up_own", up_shape, flip_feats, pre_grads, up_in, after)
            after = [up_own]
        else:
            after = give_back(after)
        up_in = send(messages)
    while len(feat_back) < peers:
        after = give_back(after)
    tokens_grad, gate_sums = pl.pallas_call(
        functools.partial(unpack_kernel, capacity, width, peers),
        in_specs=[WHOLE] * (1 + peers) + [LATER] * len(after),
        out_specs=[WHOLE] * 2,
        out_shape=[
            jax.ShapeDtypeStruct((count, width), BF16),
            jax.ShapeDtypeStruct((count, LANES), F32),
        ],
        compiler_params=params(),
        name="unpack",
    )(slot, *(feat_back[k] for k in range(peers)), *after)
    down = last_call("down_last", ring, down_own, [a for a, _, _ in down_in], [up_own])
    up = last_call("up_last", ring, up_own, [a for a, _, _ in up_in], [in_hbm(down)])
    gate_result = ((gate_sums[:, 0] + gate_sums[:, 1]) / gate_prob.astype(F32)).astype(BF16)
    return (tokens_grad, gate_result, up, down)


def solution(mesh):
    return jax.shard_map(
        per_device,
        mesh=mesh,
        in_specs=(
            P(("dp", "expert"), None),
            P(("dp", "expert"), None),
            P(("dp", "expert")),
            P(("dp", "expert")),
            P("expert", None, None),
            P("expert", None, None),
        ),
        out_specs=(
            P(("dp", "expert"), None),
            P(("dp", "expert")),
            P("expert", "dp", None),
            P("expert", "dp", None),
        ),
        check_vma=False,
    )
```

```python
import functools

import jax
import jax.numpy as jnp
from jax import lax
from jax.experimental import pallas as pl
from jax.experimental.pallas import tpu as pltpu
from jax.sharding import PartitionSpec as P

SQRT_HALF = 0.7071067811865476
INV_ROOT_TAU = 0.3989422804014327
LANES = 128
VMEM_LIMIT = 16 * 1024 * 1024
F32 = jnp.float32
BF16 = jnp.bfloat16
WHOLE = pl.BlockSpec(memory_space=pltpu.VMEM)
LATER = pl.BlockSpec(memory_space=pl.ANY)


def in_hbm(array):
    return pltpu.with_memory_space_constraint(array, pltpu.HBM)


def params(*semantics):
    return pltpu.CompilerParams(
        vmem_limit_bytes=VMEM_LIMIT, dimension_semantics=semantics or None
    )


def dot(left, right, left_dim, right_dim):
    return lax.dot_general(
        left, right, (((left_dim,), (right_dim,)), ((), ())), preferred_element_type=F32
    )


def slot_row(id_row, experts, capacity, me):
    count = id_row.shape[1]
    expert = lax.broadcasted_iota(jnp.int32, (max(experts, 8), count), 0)
    chosen = expert == id_row
    earlier = lax.broadcasted_iota(jnp.int32, (count, count), 0) < lax.broadcasted_iota(
        jnp.int32, (count, count), 1
    )
    before = dot(
        jnp.where(chosen, 1.0, 0.0).astype(BF16), jnp.where(earlier, 1.0, 0.0).astype(BF16), 1, 0
    )
    position = jnp.sum(jnp.where(chosen, before, 0.0), axis=0, keepdims=True).astype(jnp.int32)
    return (id_row ^ me) * capacity + position


def pick_rows(slot, block, capacity, value):
    row = lax.broadcasted_iota(jnp.int32, (capacity, slot.shape[1]), 0) + block * capacity
    return jnp.where(row == slot, value, 0.0).astype(BF16)


def pack_kernel(experts, capacity, near, *refs):
    sources, refs = refs[:4], refs[4:]
    slot_ref, outs = refs[0], refs[1:-5]
    held, sems = refs[-5:-1], refs[-1]
    copies = [
        pltpu.make_async_copy(source, target, sems.at[i])
        for i, (source, target) in enumerate(zip(sources, held))
    ]
    for copy in copies:
        copy.start()
    id_ref, gate_ref, grad_ref, tokens_ref = held
    copies[0].wait()
    count = id_ref.shape[0]
    slot = slot_row(id_ref[...].reshape(1, count), experts, capacity, lax.axis_index("expert"))
    slot_ref[...] = slot
    for copy in copies[1:]:
        copy.wait()
    gate = gate_ref[...].astype(F32).reshape(1, count)
    for block, out in enumerate(outs[near:]):
        out[...] = dot(pick_rows(slot, block, capacity, gate), grad_ref[...], 1, 0).astype(BF16)
    for block, out in enumerate(outs[:near]):
        out[...] = dot(pick_rows(slot, block, capacity, 1.0), tokens_ref[...], 1, 0).astype(BF16)


def repack_kernel(experts, capacity, id_ref, tokens_ref, _, *outs):
    slot = slot_row(id_ref[...], experts, capacity, lax.axis_index("expert"))
    for block, out in enumerate(outs):
        out[...] = dot(pick_rows(slot, block, capacity, 1.0), tokens_ref[...], 1, 0).astype(BF16)


def unpack_kernel(capacity, width, peers, slot_ref, *refs):
    blocks, (feat_ref, gate_ref) = refs[:peers], refs[-2:]
    slot = slot_ref[...]
    count = slot.shape[1]
    total = None
    for block, ref in enumerate(blocks):
        row = lax.broadcasted_iota(jnp.int32, (capacity, count), 0) + block * capacity
        pick = jnp.where(row == slot, 1.0, 0.0).astype(BF16)
        part = dot(pick, ref[...], 0, 0)
        total = part if total is None else total + part
    feat_ref[...] = total[:, :width].astype(BF16)
    gate_ref[...] = total[:, width:]


def call(body, inputs, out_shape, name, after=()):
    return pl.pallas_call(
        body,
        in_specs=[WHOLE] * len(inputs) + [LATER] * len(after),
        out_specs=[WHOLE] * len(out_shape),
        out_shape=[jax.ShapeDtypeStruct(*s) for s in out_shape],
        compiler_params=params(),
        name=name,
    )(*inputs, *after)


def hidden_kernel(peers, tiles, *refs):
    blocks, up_ref = refs[:peers], refs[peers]
    flip_feat_ref, hidden_ref, flip_hidden_ref, slope_ref = refs[-4:]
    feat = jnp.concatenate([ref[...] for ref in blocks], axis=0)
    flip_feat_ref[...] = feat.T
    tile = up_ref.shape[2] // tiles
    for i in range(tiles):
        part = slice(i * tile, (i + 1) * tile)
        pre_act = dot(feat, up_ref[0, :, part], 1, 0)
        cdf = 0.5 * (1.0 + lax.erf(pre_act * SQRT_HALF))
        hidden = (pre_act * cdf).astype(BF16)
        hidden_ref[:, part] = hidden
        flip_hidden_ref[part, :] = hidden.T
        slope = cdf + pre_act * jnp.exp(-0.5 * pre_act * pre_act) * INV_ROOT_TAU
        slope_ref[:, part] = slope.astype(BF16)


def hidden_call(blocks, up_weight, after=()):
    _, width, inner = up_weight.shape
    rows = len(blocks) * blocks[0].shape[0]
    return call(
        functools.partial(hidden_kernel, len(blocks), 8),
        [*blocks, up_weight],
        [
            ((width, rows), BF16),
            ((rows, inner), BF16),
            ((inner, rows), BF16),
            ((rows, inner), BF16),
        ],
        "hidden",
        after,
    )


def pre_grad_kernel(peers, tiles, *refs):
    blocks = refs[:peers]
    down_ref, hidden_ref, slope_ref = refs[peers : peers + 3]
    pre_ref, sum_ref = refs[-2:]
    scaled = jnp.concatenate([ref[...] for ref in blocks], axis=0)
    tile = down_ref.shape[1] // tiles
    total = 0.0
    for i in range(tiles):
        part = slice(i * tile, (i + 1) * tile)
        hidden_grad = dot(scaled, down_ref[0, part, :], 1, 1)
        pre_ref[:, part] = (hidden_grad * slope_ref[:, part].astype(F32)).astype(BF16)
        product = hidden_grad * hidden_ref[:, part].astype(F32)
        for j in range(tile // LANES):
            total += product[:, j * LANES : (j + 1) * LANES]
    sum_ref[...] = jnp.broadcast_to(jnp.sum(total, axis=1, keepdims=True), sum_ref.shape)


def pre_grad_call(blocks, down_weight, hidden, slope, after=()):
    _, inner, width = down_weight.shape
    rows = len(blocks) * blocks[0].shape[0]
    return call(
        functools.partial(pre_grad_kernel, len(blocks), 8),
        [*blocks, down_weight, hidden, slope],
        [((rows, inner), BF16), ((rows, LANES), F32)],
        "pre_grad",
        after,
    )


def feat_grad_kernel(block, pre_ref, up_ref, sum_ref, *refs):
    out = refs[-1]
    capacity = out.shape[0]
    part = slice(block * capacity, (block + 1) * capacity)
    width = up_ref.shape[1]
    out[:, :width] = dot(pre_ref[part, :], up_ref[0], 1, 1).astype(BF16)
    total = sum_ref[part, :]
    high = total.astype(BF16).astype(F32)
    lane = lax.broadcasted_iota(jnp.int32, total.shape, 1)
    out[:, width:] = jnp.where(lane == 0, high, total - high).astype(BF16)


def feat_grad_call(pre_grad, up_weight, sums, block, capacity, after=()):
    shape = (capacity, up_weight.shape[1] + LANES)
    return call(
        functools.partial(feat_grad_kernel, block),
        [pre_grad, up_weight, sums],
        [(shape, BF16)],
        "feat_grad",
        after,
    )[0]


def ring_chunk(step, count):
    index = lax.axis_index("dp")
    half = lax.div(index, 2)
    place = jnp.where(lax.rem(index, 2) == 0, half, count - 1 - half)
    chunks = []
    for move in (count - step, step):
        position = lax.rem(place + move, count)
        mirror = 2 * (count - 1 - position) + 1
        chunks.append(jnp.where(position < count // 2, 2 * position, mirror))
    return chunks


def ring_pairs(count):
    half = count // 2
    ring = [2 * p if p < half else 2 * (count - 1 - p) + 1 for p in range(count)]
    return [(ring[p], ring[(p + 1) % count]) for p in range(count)]


def step_kernel(parts, arrivals, step, count, *refs):
    groups = len(parts)
    lefts, refs = refs[:groups], refs[groups:]
    rights, refs = refs[: sum(parts)], refs[sum(parts) :]
    totals = [0.0, 0.0]
    chunks = ring_chunk(step, count) if groups else None
    for i, ref in enumerate(refs[:arrivals]):
        totals[i % 2] += ref[...].astype(F32)
    for left, blocks in zip(lefts, parts):
        right = [ref[...] for ref in rights[:blocks]]
        right = right[0] if blocks == 1 else jnp.concatenate(right, axis=0)
        rights = rights[blocks:]
        half = right.shape[1] // 2
        rows = left.shape[0] // count
        for way in range(2):
            start = pl.multiple_of(chunks[way] * rows, rows)
            totals[way] += dot(
                left[pl.ds(start, rows), :], right[:, way * half : (way + 1) * half], 1, 0
            )
    for way, out in enumerate(refs[-2:]):
        out[...] = totals[way].astype(out.dtype)


def last_kernel(way, count, arrived_ref, own_ref, *refs):
    out, held, sem = refs[-3:]
    half = held.shape[1]
    held[...] = (own_ref[...] + arrived_ref[...].astype(F32)) * (1.0 / count)
    copy = pltpu.make_async_copy(held, out.at[0, :, way * half : (way + 1) * half], sem)
    copy.start()
    copy.wait()


def last_call(name, count, arrived, own, after):
    rows, half = own[0].shape
    out = []
    for way in range(2):
        out = [
            pl.pallas_call(
                functools.partial(last_kernel, way, count),
                in_specs=[WHOLE] * 2
                + [pl.BlockSpec(memory_space=pltpu.HBM)] * len(out)
                + [LATER] * len(after),
                out_specs=pl.BlockSpec(memory_space=pltpu.HBM),
                out_shape=pltpu.HBM((1, rows, 2 * half), F32),
                input_output_aliases={2: 0} if out else {},
                scratch_shapes=[pltpu.VMEM((rows, half), F32), pltpu.SemaphoreType.DMA],
                compiler_params=params(),
                name=name,
            )(arrived[way], own[way], *(in_hbm(a) for a in out), *after)
        ]
        after = []
    return out[0]


def ring_step(name, step, count, shape, lefts, rights, arrived, after=(), dtype=BF16):
    blocks = [block for group in rights for block in group]
    inputs = [*lefts, *blocks, *arrived]
    return pl.pallas_call(
        functools.partial(step_kernel, [len(group) for group in rights], len(arrived), step, count),
        in_specs=[WHOLE] * len(inputs) + [LATER] * len(after),
        out_specs=[WHOLE] * 2,
        out_shape=[jax.ShapeDtypeStruct(shape, dtype)] * 2,
        compiler_params=params(),
        name=name,
    )(*inputs, *after)


def per_device(tokens, out_grad, gate_prob, expert_id, up_weight, down_weight):
    count, width = tokens.shape
    inner = up_weight.shape[2]
    peers = lax.axis_size("expert")
    experts = peers * up_weight.shape[0]
    capacity = 2 * count // experts
    ring = lax.axis_size("dp")
    sources = [[(i, i ^ k) for i in range(peers)] for k in range(peers)]
    forward = ring_pairs(ring)
    backward = [(b, a) for a, b in forward]

    def exchange(outs, reach):
        return {k: lax.ppermute(outs[k], "expert", sources[k]) for k in reach}

    near, far = range(1, peers // 2), range(peers // 2, peers)
    hbm = pl.BlockSpec(memory_space=pltpu.HBM)
    across = [(i, i ^ peers // 2) for i in range(peers)]
    tokens_across = lax.ppermute(tokens, "expert", across)
    id_across = lax.ppermute(expert_id.reshape(1, count), "expert", across)

    block_shape = jax.ShapeDtypeStruct((capacity, width), BF16)
    slot, *packed = pl.pallas_call(
        functools.partial(pack_kernel, experts, capacity, peers // 2),
        in_specs=[hbm] * 4,
        out_specs=[WHOLE] * (1 + peers // 2 + peers),
        out_shape=[jax.ShapeDtypeStruct((1, count), jnp.int32)]
        + [block_shape] * (peers // 2 + peers),
        scratch_shapes=[
            pltpu.VMEM((count,), jnp.int32),
            pltpu.VMEM((count,), BF16),
            pltpu.VMEM((count, width), BF16),
            pltpu.VMEM((count, width), BF16),
            pltpu.SemaphoreType.DMA((4,)),
        ],
        compiler_params=params(),
        name="pack",
    )(*(in_hbm(a) for a in (expert_id, gate_prob, out_grad, tokens)))
    feat_out, grad_out = packed[: peers // 2], packed[peers // 2 :]
    grad_in = {0: grad_out[0], **exchange(grad_out, far), **exchange(grad_out, near)}
    feat_in = {0: feat_out[0], **exchange(feat_out, near)}
    groups = [[0, *near], [peers // 2], [*far][1:]]
    groups = [group for group in groups if group]
    scaleds = [[grad_in[k] for k in group] for group in groups]
    hiddens, pre_grads, sums = [], [], []

    def add_hidden(blocks, after=()):
        hiddens.append(hidden_call(blocks, up_weight, after))
        return [hiddens[-1][1]]

    def add_pre_grad(after=()):
        group = len(pre_grads)
        _, hidden, _, slope = hiddens[group]
        pre, total = pre_grad_call(scaleds[group], down_weight, hidden, slope, after)
        pre_grads.append([pre])
        sums.append(total)
        return [total]

    add_hidden([feat_in[k] for k in groups[0]])
    after = add_pre_grad()
    across_out = pl.pallas_call(
        functools.partial(repack_kernel, experts, capacity),
        in_specs=[WHOLE, WHOLE, LATER],
        out_specs=[WHOLE] * (peers // 2),
        out_shape=[block_shape] * (peers // 2),
        compiler_params=params(),
        name="repack",
    )(id_across, tokens_across, *after)
    across_in = exchange(across_out, near)
    after = add_hidden(across_out[:1])
    if len(groups) > 2:
        after = add_pre_grad(after)
        after = add_hidden([across_in[k] for k in near], after)
    flip_feats = [part[0] for part in hiddens]
    flip_hiddens = [part[2] for part in hiddens]
    down_shape = (inner // ring, width // 2)
    up_shape = (width // ring, inner // 2)
    down_in = ring_step(
        "down_early",
        1,
        ring,
        down_shape,
        flip_hiddens[:-1],
        scaleds[:-1],
        [],
        after,
        F32,
    )

    def send(pair):
        return [lax.ppermute(pair[0], "dp", forward), lax.ppermute(pair[1], "dp", backward)]

    turn = 1 if ring < 8 else 2
    span = min(4, ring - turn)
    returns = [*far, *near, 0]
    feat_back = {}
    up_in, after, landed = [], [], []
    for step in range(1, ring):
        late = slice(-1, None) if step == 1 else slice(None)
        down = ring_step(
            "down_step",
                step,
            ring,
            down_shape,
            flip_hiddens[late],
            scaleds[late],
            down_in,
            after,
        )
        down_in = send(down)
        after = [*down]
        if step == 1:
            after = add_pre_grad(after)
        up = ring_step(
            "up_step", step, ring, up_shape, flip_feats, pre_grads, up_in, after
        )
        up_in = send(up)
        after = [*up] + landed
        landed = []
        first = (step - turn) * len(returns) // span
        stop = (step - turn + 1) * len(returns) // span
        for k in returns[max(first, 0) : max(stop, 0)]:
            group = [k in members for members in groups].index(True)
            block = feat_grad_call(
                pre_grads[group][0],
                up_weight,
                sums[group],
                groups[group].index(k),
                capacity,
                after,
            )
            after = [block]
            feat_back[k] = lax.ppermute(block, "expert", sources[k]) if k else block
            landed.append(feat_back[k])
        if step == max(ring - 2, 1):
            down_last = ring_step(
                "down_own",
                        ring,
                ring,
                down_shape,
                flip_hiddens,
                scaleds,
                [],
                after,
                F32,
            )
            up_last = ring_step(
                "up_own",
                        ring,
                ring,
                up_shape,
                flip_feats,
                pre_grads,
                [],
                down_last[:1],
                F32,
            )
            after = up_last[:1]
    down = last_call("down_last", ring, down_in, down_last, [])
    up = last_call("up_last", ring, up_in, up_last, [in_hbm(down)])
    tokens_grad, gate_sums = pl.pallas_call(
        functools.partial(unpack_kernel, capacity, width, peers),
        in_specs=[WHOLE] * (1 + peers) + [LATER] * len(after),
        out_specs=[WHOLE] * 2,
        out_shape=[
            jax.ShapeDtypeStruct((count, width), BF16),
            jax.ShapeDtypeStruct((count, LANES), F32),
        ],
        compiler_params=params(),
        name="unpack",
    )(slot, *(feat_back[k] for k in range(peers)), *after)
    gate_result = ((gate_sums[:, 0] + gate_sums[:, 1]) / gate_prob.astype(F32)).astype(BF16)
    return (tokens_grad, gate_result, up, down)


def solution(mesh):
    return jax.shard_map(
        per_device,
        mesh=mesh,
        in_specs=(
            P(("dp", "expert"), None),
            P(("dp", "expert"), None),
            P(("dp", "expert")),
            P(("dp", "expert")),
            P("expert", None, None),
            P("expert", None, None),
        ),
        out_specs=(
            P(("dp", "expert"), None),
            P(("dp", "expert")),
            P("expert", "dp", None),
            P("expert", "dp", None),
        ),
        check_vma=False,
    )
```

```python
import functools

import jax
import jax.numpy as jnp
from jax import lax
from jax.experimental import pallas as pl
from jax.experimental.pallas import tpu as pltpu
from jax.sharding import PartitionSpec as P

SQRT_HALF = 0.7071067811865476
INV_ROOT_TAU = 0.3989422804014327
LANES = 128
VMEM_LIMIT = 16 * 1024 * 1024
F32 = jnp.float32
BF16 = jnp.bfloat16
WHOLE = pl.BlockSpec(memory_space=pltpu.VMEM)
LATER = pl.BlockSpec(memory_space=pl.ANY)


def in_hbm(array):
    return pltpu.with_memory_space_constraint(array, pltpu.HBM)


def params(*semantics):
    return pltpu.CompilerParams(
        vmem_limit_bytes=VMEM_LIMIT, dimension_semantics=semantics or None
    )


def dot(left, right, left_dim, right_dim):
    return lax.dot_general(
        left, right, (((left_dim,), (right_dim,)), ((), ())), preferred_element_type=F32
    )


def slot_row(id_row, experts, capacity, me):
    count = id_row.shape[1]
    expert = lax.broadcasted_iota(jnp.int32, (max(experts, 8), count), 0)
    chosen = expert == id_row
    earlier = lax.broadcasted_iota(jnp.int32, (count, count), 0) < lax.broadcasted_iota(
        jnp.int32, (count, count), 1
    )
    before = dot(
        jnp.where(chosen, 1.0, 0.0).astype(BF16), jnp.where(earlier, 1.0, 0.0).astype(BF16), 1, 0
    )
    position = jnp.sum(jnp.where(chosen, before, 0.0), axis=0, keepdims=True).astype(jnp.int32)
    return (id_row ^ me) * capacity + position


def pick_rows(slot, block, capacity, value):
    row = lax.broadcasted_iota(jnp.int32, (capacity, slot.shape[1]), 0) + block * capacity
    return jnp.where(row == slot, value, 0.0).astype(BF16)


def pack_kernel(experts, capacity, near, *refs):
    sources, refs = refs[:4], refs[4:]
    slot_ref, outs = refs[0], refs[1:-5]
    held, sems = refs[-5:-1], refs[-1]
    copies = [
        pltpu.make_async_copy(source, target, sems.at[i])
        for i, (source, target) in enumerate(zip(sources, held))
    ]
    for copy in copies:
        copy.start()
    id_ref, gate_ref, grad_ref, tokens_ref = held
    copies[0].wait()
    count = id_ref.shape[0]
    slot = slot_row(id_ref[...].reshape(1, count), experts, capacity, lax.axis_index("expert"))
    slot_ref[...] = slot
    for copy in copies[1:]:
        copy.wait()
    gate = gate_ref[...].astype(F32).reshape(1, count)
    for block, out in enumerate(outs[near:]):
        out[...] = dot(pick_rows(slot, block, capacity, gate), grad_ref[...], 1, 0).astype(BF16)
    for block, out in enumerate(outs[:near]):
        out[...] = dot(pick_rows(slot, block, capacity, 1.0), tokens_ref[...], 1, 0).astype(BF16)


def repack_kernel(experts, capacity, id_ref, tokens_ref, _, *outs):
    slot = slot_row(id_ref[...], experts, capacity, lax.axis_index("expert"))
    for block, out in enumerate(outs):
        out[...] = dot(pick_rows(slot, block, capacity, 1.0), tokens_ref[...], 1, 0).astype(BF16)


def unpack_kernel(capacity, width, peers, slot_ref, *refs):
    blocks, (feat_ref, gate_ref) = refs[:peers], refs[-2:]
    slot = slot_ref[...]
    count = slot.shape[1]
    total = None
    for block, ref in enumerate(blocks):
        row = lax.broadcasted_iota(jnp.int32, (capacity, count), 0) + block * capacity
        pick = jnp.where(row == slot, 1.0, 0.0).astype(BF16)
        part = dot(pick, ref[...], 0, 0)
        total = part if total is None else total + part
    feat_ref[...] = total[:, :width].astype(BF16)
    gate_ref[...] = total[:, width:]


def call(body, inputs, out_shape, name, after=()):
    return pl.pallas_call(
        body,
        in_specs=[WHOLE] * len(inputs) + [LATER] * len(after),
        out_specs=[WHOLE] * len(out_shape),
        out_shape=[jax.ShapeDtypeStruct(*s) for s in out_shape],
        compiler_params=params(),
        name=name,
    )(*inputs, *after)


def hidden_kernel(peers, tiles, *refs):
    blocks, up_ref = refs[:peers], refs[peers]
    flip_feat_ref, hidden_ref, flip_hidden_ref, slope_ref = refs[-4:]
    feat = jnp.concatenate([ref[...] for ref in blocks], axis=0)
    flip_feat_ref[...] = feat.T
    tile = up_ref.shape[2] // tiles
    for i in range(tiles):
        part = slice(i * tile, (i + 1) * tile)
        pre_act = dot(feat, up_ref[0, :, part], 1, 0)
        cdf = 0.5 * (1.0 + lax.erf(pre_act * SQRT_HALF))
        hidden = (pre_act * cdf).astype(BF16)
        hidden_ref[:, part] = hidden
        flip_hidden_ref[part, :] = hidden.T
        slope = cdf + pre_act * jnp.exp(-0.5 * pre_act * pre_act) * INV_ROOT_TAU
        slope_ref[:, part] = slope.astype(BF16)


def hidden_call(blocks, up_weight, after=()):
    _, width, inner = up_weight.shape
    rows = len(blocks) * blocks[0].shape[0]
    return call(
        functools.partial(hidden_kernel, len(blocks), 8),
        [*blocks, up_weight],
        [
            ((width, rows), BF16),
            ((rows, inner), BF16),
            ((inner, rows), BF16),
            ((rows, inner), BF16),
        ],
        "hidden",
        after,
    )


def pre_grad_kernel(peers, tiles, *refs):
    blocks = refs[:peers]
    down_ref, hidden_ref, slope_ref = refs[peers : peers + 3]
    pre_ref, sum_ref = refs[-2:]
    scaled = jnp.concatenate([ref[...] for ref in blocks], axis=0)
    tile = down_ref.shape[1] // tiles
    total = 0.0
    for i in range(tiles):
        part = slice(i * tile, (i + 1) * tile)
        hidden_grad = dot(scaled, down_ref[0, part, :], 1, 1)
        pre_ref[:, part] = (hidden_grad * slope_ref[:, part].astype(F32)).astype(BF16)
        product = hidden_grad * hidden_ref[:, part].astype(F32)
        for j in range(tile // LANES):
            total += product[:, j * LANES : (j + 1) * LANES]
    sum_ref[...] = jnp.broadcast_to(jnp.sum(total, axis=1, keepdims=True), sum_ref.shape)


def pre_grad_call(blocks, down_weight, hidden, slope, after=()):
    _, inner, width = down_weight.shape
    rows = len(blocks) * blocks[0].shape[0]
    return call(
        functools.partial(pre_grad_kernel, len(blocks), 8),
        [*blocks, down_weight, hidden, slope],
        [((rows, inner), BF16), ((rows, LANES), F32)],
        "pre_grad",
        after,
    )


def feat_grad_kernel(block, pre_ref, up_ref, sum_ref, *refs):
    out = refs[-1]
    capacity = out.shape[0]
    part = slice(block * capacity, (block + 1) * capacity)
    width = up_ref.shape[1]
    out[:, :width] = dot(pre_ref[part, :], up_ref[0], 1, 1).astype(BF16)
    total = sum_ref[part, :]
    high = total.astype(BF16).astype(F32)
    lane = lax.broadcasted_iota(jnp.int32, total.shape, 1)
    out[:, width:] = jnp.where(lane == 0, high, total - high).astype(BF16)


def feat_grad_call(pre_grad, up_weight, sums, block, capacity, after=()):
    shape = (capacity, up_weight.shape[1] + LANES)
    return call(
        functools.partial(feat_grad_kernel, block),
        [pre_grad, up_weight, sums],
        [(shape, BF16)],
        "feat_grad",
        after,
    )[0]


def ring_chunk(offset, count):
    index = lax.axis_index("dp")
    half = lax.div(index, 2)
    place = jnp.where(lax.rem(index, 2) == 0, half, count - 1 - half)
    position = lax.rem(place + (offset + count), count)
    mirror = 2 * (count - 1 - position) + 1
    return jnp.where(position < count // 2, 2 * position, mirror)


def ring_targets(step, count):
    targets = []
    for way, sign in ((0, 1), (1, -1)):
        for side in range(2):
            offset = count // 2 - step + (side == way)
            if offset > 0:
                targets.append(((way, side), sign * offset))
    return targets


def ring_pairs(count):
    half = count // 2
    ring = [2 * p if p < half else 2 * (count - 1 - p) + 1 for p in range(count)]
    return [(ring[p], ring[(p + 1) % count]) for p in range(count)]


def step_kernel(parts, arrivals, targets, count, half, *refs):
    groups = len(parts)
    lefts, refs = refs[:groups], refs[groups:]
    rights, refs = refs[: sum(parts)], refs[sum(parts) :]
    totals = {key: 0.0 for key, _ in targets}
    for ref, (way, sides) in zip(refs, arrivals):
        for i, side in enumerate(sides):
            if (way, side) in totals:
                totals[way, side] += ref[:, i * half : (i + 1) * half].astype(F32)
    for left, blocks in zip(lefts, parts):
        rows = left.shape[0] // count
        for side in range(2):
            wanted = [(key, offset) for key, offset in targets if key[1] == side]
            if not wanted:
                continue
            right = [
                ref[...] if ref.shape[1] == half else ref[:, side * half : (side + 1) * half]
                for ref in rights[:blocks]
            ]
            right = right[0] if blocks == 1 else jnp.concatenate(right, axis=0)
            picked = []
            for _, offset in wanted:
                start = pl.multiple_of(ring_chunk(offset, count) * rows, rows)
                picked.append(left[pl.ds(start, rows), :])
            picked = picked[0] if len(picked) == 1 else jnp.concatenate(picked, axis=0)
            product = dot(picked, right, 1, 0)
            for i, (key, _) in enumerate(wanted):
                totals[key] += product[i * rows : (i + 1) * rows]
        rights = rights[blocks:]
    ways = sorted({way for way, _ in totals})
    for way, out in zip(ways, refs[-len(ways) :]):
        for i, key in enumerate(sorted(key for key in totals if key[0] == way)):
            out[:, i * half : (i + 1) * half] = totals[key].astype(out.dtype)


def ring_step(name, targets, count, shape, lefts, rights, arrived, after=(), dtype=BF16):
    rows, half = shape
    held = {}
    for way, side in sorted(key for key, _ in targets):
        held.setdefault(way, []).append(side)
    blocks = [block for group in rights for block in group]
    outs = call(
        functools.partial(
            step_kernel,
            [len(group) for group in rights],
            [(way, sides) for _, way, sides in arrived],
            targets,
            count,
            half,
        ),
        [*lefts, *blocks, *(array for array, _, _ in arrived)],
        [((rows, half * len(sides)), dtype) for sides in held.values()],
        name,
        after,
    )
    return [(out, way, tuple(sides)) for out, (way, sides) in zip(outs, held.items())]


def last_kernel(way, count, arrived_ref, own_ref, *refs):
    out, held, sem = refs[-3:]
    half = held.shape[1]
    own = own_ref[:, way * half : (way + 1) * half]
    held[...] = (own + arrived_ref[...].astype(F32)) * (1.0 / count)
    copy = pltpu.make_async_copy(held, out.at[0, :, way * half : (way + 1) * half], sem)
    copy.start()
    copy.wait()


def last_call(name, count, arrived, own, after):
    rows, half = own.shape[0], own.shape[1] // 2
    out = []
    for way in range(2):
        out = [
            pl.pallas_call(
                functools.partial(last_kernel, way, count),
                in_specs=[WHOLE] * 2
                + [pl.BlockSpec(memory_space=pltpu.HBM)] * len(out)
                + [LATER] * len(after),
                out_specs=pl.BlockSpec(memory_space=pltpu.HBM),
                out_shape=pltpu.HBM((1, rows, 2 * half), F32),
                input_output_aliases={2: 0} if out else {},
                scratch_shapes=[pltpu.VMEM((rows, half), F32), pltpu.SemaphoreType.DMA],
                compiler_params=params(),
                name=name,
            )(arrived[way], own, *(in_hbm(a) for a in out), *after)
        ]
        after = []
    return out[0]


def per_device(tokens, out_grad, gate_prob, expert_id, up_weight, down_weight):
    count, width = tokens.shape
    inner = up_weight.shape[2]
    peers = lax.axis_size("expert")
    experts = peers * up_weight.shape[0]
    capacity = 2 * count // experts
    ring = lax.axis_size("dp")
    sources = [[(i, i ^ k) for i in range(peers)] for k in range(peers)]
    forward = ring_pairs(ring)
    backward = [(b, a) for a, b in forward]

    def exchange(outs, reach):
        return {k: lax.ppermute(outs[k], "expert", sources[k]) for k in reach}

    near, far = range(1, peers // 2), range(peers // 2, peers)
    hbm = pl.BlockSpec(memory_space=pltpu.HBM)
    across = [(i, i ^ peers // 2) for i in range(peers)]
    tokens_across = lax.ppermute(tokens, "expert", across)
    id_across = lax.ppermute(expert_id.reshape(1, count), "expert", across)

    block_shape = jax.ShapeDtypeStruct((capacity, width), BF16)
    slot, *packed = pl.pallas_call(
        functools.partial(pack_kernel, experts, capacity, peers // 2),
        in_specs=[hbm] * 4,
        out_specs=[WHOLE] * (1 + peers // 2 + peers),
        out_shape=[jax.ShapeDtypeStruct((1, count), jnp.int32)]
        + [block_shape] * (peers // 2 + peers),
        scratch_shapes=[
            pltpu.VMEM((count,), jnp.int32),
            pltpu.VMEM((count,), BF16),
            pltpu.VMEM((count, width), BF16),
            pltpu.VMEM((count, width), BF16),
            pltpu.SemaphoreType.DMA((4,)),
        ],
        compiler_params=params(),
        name="pack",
    )(*(in_hbm(a) for a in (expert_id, gate_prob, out_grad, tokens)))
    feat_out, grad_out = packed[: peers // 2], packed[peers // 2 :]
    grad_in = {0: grad_out[0], **exchange(grad_out, far), **exchange(grad_out, near)}
    feat_in = {0: feat_out[0], **exchange(feat_out, near)}
    groups = [[0, *near], [peers // 2], [*far][1:]]
    groups = [group for group in groups if group]
    scaleds = [[grad_in[k] for k in group] for group in groups]
    hiddens, pre_grads, sums = [], [], []

    def add_hidden(blocks, after=()):
        hiddens.append(hidden_call(blocks, up_weight, after))
        return [hiddens[-1][1]]

    def add_pre_grad(after=()):
        group = len(pre_grads)
        _, hidden, _, slope = hiddens[group]
        pre, total = pre_grad_call(scaleds[group], down_weight, hidden, slope, after)
        pre_grads.append([pre])
        sums.append(total)
        return [total]

    add_hidden([feat_in[k] for k in groups[0]])
    after = add_pre_grad()
    across_out = pl.pallas_call(
        functools.partial(repack_kernel, experts, capacity),
        in_specs=[WHOLE, WHOLE, LATER],
        out_specs=[WHOLE] * (peers // 2),
        out_shape=[block_shape] * (peers // 2),
        compiler_params=params(),
        name="repack",
    )(id_across, tokens_across, *after)
    across_in = exchange(across_out, near)
    after = add_hidden(across_out[:1])
    if len(groups) > 2:
        after = add_pre_grad(after)
        after = add_hidden([across_in[k] for k in near], after)
    flip_feats = [part[0] for part in hiddens]
    flip_hiddens = [part[2] for part in hiddens]
    down_shape = (inner // ring, width // 2)
    up_shape = (width // ring, inner // 2)
    early = ring_step(
        "down_early",
        ring_targets(1, ring),
        ring,
        down_shape,
        flip_hiddens[:-1],
        scaleds[:-1],
        [],
        after,
        F32,
    )
    after = [early[0][0]]

    def send(messages):
        ways = (forward, backward)
        return [(lax.ppermute(a, "dp", ways[way]), way, sides) for a, way, sides in messages]

    hops = ring // 2
    returns = [*far, *near, 0]
    spread = max(min(4, 2 * hops - 2), 1)
    feat_back, landed, slots = {}, [], []

    def give_back(after):
        slots.append(0)
        first = (len(slots) - 1) * len(returns) // spread
        stop = len(slots) * len(returns) // spread
        after = [*after, *landed]
        landed.clear()
        for k in returns[first:stop]:
            group = [k in members for members in groups].index(True)
            block = feat_grad_call(
                pre_grads[group][0],
                up_weight,
                sums[group],
                groups[group].index(k),
                capacity,
                after,
            )
            after = [block]
            feat_back[k] = lax.ppermute(block, "expert", sources[k]) if k else block
            landed.append(feat_back[k])
        return after

    def own(name, shape, lefts, rights, arrived, after):
        done = [
            (a, 0, tuple(None if side == way else side for side in sides))
            for a, way, sides in arrived
        ]
        targets = [((0, 0), 0), ((0, 1), 0)]
        return ring_step(name, targets, ring, shape, lefts, rights, done, after, F32)[0][0]

    down_in, up_in = [], []
    for step in range(1, hops + 1):
        targets = ring_targets(step, ring)
        if step == 1:
            messages = ring_step(
                "down_step",
                targets,
                ring,
                down_shape,
                flip_hiddens[-1:],
                scaleds[-1:],
                early,
                after,
            )
            down_in = send(messages)
            after = add_pre_grad([a for a, _, _ in messages])
        else:
            messages = ring_step(
                "down_step", targets, ring, down_shape, flip_hiddens, scaleds, down_in, after
            )
            after = [a for a, _, _ in messages]
            if step == hops:
                down_own = own(
                    "down_own", down_shape, flip_hiddens, scaleds, down_in, after
                )
                after = [down_own]
            else:
                after = give_back(after)
            down_in = send(messages)
        messages = ring_step(
            "up_step", targets, ring, up_shape, flip_feats, pre_grads, up_in, after
        )
        after = [a for a, _, _ in messages]
        if step == hops:
            up_own = own("up_own", up_shape, flip_feats, pre_grads, up_in, after)
            after = [up_own]
        else:
            after = give_back(after)
        up_in = send(messages)
    while len(feat_back) < peers:
        after = give_back(after)
    tokens_grad, gate_sums = pl.pallas_call(
        functools.partial(unpack_kernel, capacity, width, peers),
        in_specs=[WHOLE] * (1 + peers) + [LATER] * len(after),
        out_specs=[WHOLE] * 2,
        out_shape=[
            jax.ShapeDtypeStruct((count, width), BF16),
            jax.ShapeDtypeStruct((count, LANES), F32),
        ],
        compiler_params=params(),
        name="unpack",
    )(slot, *(feat_back[k] for k in range(peers)), *after)
    down = last_call("down_last", ring, [a for a, _, _ in down_in], down_own, [up_own])
    up = last_call("up_last", ring, [a for a, _, _ in up_in], up_own, [in_hbm(down)])
    gate_result = ((gate_sums[:, 0] + gate_sums[:, 1]) / gate_prob.astype(F32)).astype(BF16)
    return (tokens_grad, gate_result, up, down)


def solution(mesh):
    return jax.shard_map(
        per_device,
        mesh=mesh,
        in_specs=(
            P(("dp", "expert"), None),
            P(("dp", "expert"), None),
            P(("dp", "expert")),
            P(("dp", "expert")),
            P("expert", None, None),
            P("expert", None, None),
        ),
        out_specs=(
            P(("dp", "expert"), None),
            P(("dp", "expert")),
            P("expert", "dp", None),
            P("expert", "dp", None),
        ),
        check_vma=False,
    )
```

```python
import functools

import jax
import jax.numpy as jnp
from jax import lax
from jax.experimental import pallas as pl
from jax.experimental.pallas import tpu as pltpu
from jax.sharding import PartitionSpec as P

SQRT_HALF = 0.7071067811865476
INV_ROOT_TAU = 0.3989422804014327
LANES = 128
PIECES = 4
VMEM_LIMIT = 16 * 1024 * 1024
F32 = jnp.float32
BF16 = jnp.bfloat16
WHOLE = pl.BlockSpec(memory_space=pltpu.VMEM)
LATER = pl.BlockSpec(memory_space=pl.ANY)


def in_hbm(array):
    return pltpu.with_memory_space_constraint(array, pltpu.HBM)


def params(*semantics):
    return pltpu.CompilerParams(
        vmem_limit_bytes=VMEM_LIMIT, dimension_semantics=semantics or None
    )


def dot(left, right, left_dim, right_dim):
    return lax.dot_general(
        left, right, (((left_dim,), (right_dim,)), ((), ())), preferred_element_type=F32
    )


def slot_row(id_row, experts, capacity, me):
    count = id_row.shape[1]
    expert = lax.broadcasted_iota(jnp.int32, (max(experts, 8), count), 0)
    chosen = expert == id_row
    earlier = lax.broadcasted_iota(jnp.int32, (count, count), 0) < lax.broadcasted_iota(
        jnp.int32, (count, count), 1
    )
    before = dot(
        jnp.where(chosen, 1.0, 0.0).astype(BF16), jnp.where(earlier, 1.0, 0.0).astype(BF16), 1, 0
    )
    position = jnp.sum(jnp.where(chosen, before, 0.0), axis=0, keepdims=True).astype(jnp.int32)
    return (id_row ^ me) * capacity + position


def pick_rows(slot, block, capacity, value):
    row = lax.broadcasted_iota(jnp.int32, (capacity, slot.shape[1]), 0) + block * capacity
    return jnp.where(row == slot, value, 0.0).astype(BF16)


def pack_kernel(experts, capacity, near, *refs):
    sources, refs = refs[:4], refs[4:]
    slot_ref, outs = refs[0], refs[1:-5]
    held, sems = refs[-5:-1], refs[-1]
    copies = [
        pltpu.make_async_copy(source, target, sems.at[i])
        for i, (source, target) in enumerate(zip(sources, held))
    ]
    for copy in copies:
        copy.start()
    id_ref, gate_ref, grad_ref, tokens_ref = held
    copies[0].wait()
    count = id_ref.shape[0]
    slot = slot_row(id_ref[...].reshape(1, count), experts, capacity, lax.axis_index("expert"))
    slot_ref[...] = slot
    for copy in copies[1:]:
        copy.wait()
    gate = gate_ref[...].astype(F32).reshape(1, count)
    for block, out in enumerate(outs[near:]):
        out[...] = dot(pick_rows(slot, block, capacity, gate), grad_ref[...], 1, 0).astype(BF16)
    for block, out in enumerate(outs[:near]):
        out[...] = dot(pick_rows(slot, block, capacity, 1.0), tokens_ref[...], 1, 0).astype(BF16)


def repack_kernel(experts, capacity, id_ref, tokens_ref, _, *outs):
    slot = slot_row(id_ref[...], experts, capacity, lax.axis_index("expert"))
    for block, out in enumerate(outs):
        out[...] = dot(pick_rows(slot, block, capacity, 1.0), tokens_ref[...], 1, 0).astype(BF16)


def unpack_kernel(capacity, width, peers, slot_ref, *refs):
    blocks, (feat_ref, gate_ref) = refs[:peers], refs[-2:]
    slot = slot_ref[...]
    count = slot.shape[1]
    total = None
    for block, ref in enumerate(blocks):
        row = lax.broadcasted_iota(jnp.int32, (capacity, count), 0) + block * capacity
        pick = jnp.where(row == slot, 1.0, 0.0).astype(BF16)
        part = dot(pick, ref[...], 0, 0)
        total = part if total is None else total + part
    feat_ref[...] = total[:, :width].astype(BF16)
    gate_ref[...] = total[:, width:]


def call(body, inputs, out_shape, name, after=()):
    return pl.pallas_call(
        body,
        in_specs=[WHOLE] * len(inputs) + [LATER] * len(after),
        out_specs=[WHOLE] * len(out_shape),
        out_shape=[jax.ShapeDtypeStruct(*s) for s in out_shape],
        compiler_params=params(),
        name=name,
    )(*inputs, *after)


def hidden_kernel(peers, tiles, *refs):
    blocks, up_ref = refs[:peers], refs[peers]
    flip_feat_ref, hidden_ref, flip_hidden_ref, slope_ref = refs[-4:]
    feat = jnp.concatenate([ref[...] for ref in blocks], axis=0)
    flip_feat_ref[...] = feat.T
    tile = up_ref.shape[2] // tiles
    for i in range(tiles):
        part = slice(i * tile, (i + 1) * tile)
        pre_act = dot(feat, up_ref[0, :, part], 1, 0)
        cdf = 0.5 * (1.0 + lax.erf(pre_act * SQRT_HALF))
        hidden = (pre_act * cdf).astype(BF16)
        hidden_ref[:, part] = hidden
        flip_hidden_ref[part, :] = hidden.T
        slope = cdf + pre_act * jnp.exp(-0.5 * pre_act * pre_act) * INV_ROOT_TAU
        slope_ref[:, part] = slope.astype(BF16)


def hidden_call(blocks, up_weight, after=()):
    _, width, inner = up_weight.shape
    rows = len(blocks) * blocks[0].shape[0]
    return call(
        functools.partial(hidden_kernel, len(blocks), 8),
        [*blocks, up_weight],
        [
            ((width, rows), BF16),
            ((rows, inner), BF16),
            ((inner, rows), BF16),
            ((rows, inner), BF16),
        ],
        "hidden",
        after,
    )


def pre_grad_kernel(peers, tiles, *refs):
    blocks = refs[:peers]
    down_ref, hidden_ref, slope_ref = refs[peers : peers + 3]
    pre_ref, sum_ref = refs[-2:]
    scaled = jnp.concatenate([ref[...] for ref in blocks], axis=0)
    tile = down_ref.shape[1] // tiles
    total = 0.0
    for i in range(tiles):
        part = slice(i * tile, (i + 1) * tile)
        hidden_grad = dot(scaled, down_ref[0, part, :], 1, 1)
        pre_ref[:, part] = (hidden_grad * slope_ref[:, part].astype(F32)).astype(BF16)
        product = hidden_grad * hidden_ref[:, part].astype(F32)
        for j in range(tile // LANES):
            total += product[:, j * LANES : (j + 1) * LANES]
    sum_ref[...] = jnp.broadcast_to(jnp.sum(total, axis=1, keepdims=True), sum_ref.shape)


def pre_grad_call(blocks, down_weight, hidden, slope, after=()):
    _, inner, width = down_weight.shape
    rows = len(blocks) * blocks[0].shape[0]
    return call(
        functools.partial(pre_grad_kernel, len(blocks), 8),
        [*blocks, down_weight, hidden, slope],
        [((rows, inner), BF16), ((rows, LANES), F32)],
        "pre_grad",
        after,
    )


def feat_grad_kernel(block, pre_ref, up_ref, sum_ref, *refs):
    out = refs[-1]
    capacity = out.shape[0]
    part = slice(block * capacity, (block + 1) * capacity)
    width = up_ref.shape[1]
    out[:, :width] = dot(pre_ref[part, :], up_ref[0], 1, 1).astype(BF16)
    total = sum_ref[part, :]
    high = total.astype(BF16).astype(F32)
    lane = lax.broadcasted_iota(jnp.int32, total.shape, 1)
    out[:, width:] = jnp.where(lane == 0, high, total - high).astype(BF16)


def feat_grad_call(pre_grad, up_weight, sums, block, capacity, after=()):
    shape = (capacity, up_weight.shape[1] + LANES)
    return call(
        functools.partial(feat_grad_kernel, block),
        [pre_grad, up_weight, sums],
        [(shape, BF16)],
        "feat_grad",
        after,
    )[0]


def ring_chunk(step, count):
    index = lax.axis_index("dp")
    half = lax.div(index, 2)
    place = jnp.where(lax.rem(index, 2) == 0, half, count - 1 - half)
    chunks = []
    for move in (count - step, step):
        position = lax.rem(place + move, count)
        mirror = 2 * (count - 1 - position) + 1
        chunks.append(jnp.where(position < count // 2, 2 * position, mirror))
    return chunks


def ring_pairs(count):
    half = count // 2
    ring = [2 * p if p < half else 2 * (count - 1 - p) + 1 for p in range(count)]
    return [(ring[p], ring[(p + 1) % count]) for p in range(count)]


def step_kernel(parts, arrivals, step, count, *refs):
    groups = len(parts)
    lefts, refs = refs[:groups], refs[groups:]
    rights, refs = refs[: sum(parts)], refs[sum(parts) :]
    totals = [0.0, 0.0]
    chunks = ring_chunk(step, count) if groups else None
    for i, ref in enumerate(refs[:arrivals]):
        totals[i % 2] += ref[...].astype(F32)
    for left, blocks in zip(lefts, parts):
        right = [ref[...] for ref in rights[:blocks]]
        right = right[0] if blocks == 1 else jnp.concatenate(right, axis=0)
        rights = rights[blocks:]
        half = right.shape[1] // 2
        rows = left.shape[0] // count
        for way in range(2):
            start = pl.multiple_of(chunks[way] * rows, rows)
            totals[way] += dot(
                left[pl.ds(start, rows), :], right[:, way * half : (way + 1) * half], 1, 0
            )
    for way, out in enumerate(refs[-2:]):
        out[...] = totals[way].astype(out.dtype)


def last_kernel(way, count, arrived_ref, own_ref, *refs):
    out, held, sems = refs[-3:]
    rows, half = held.shape
    copies = []
    for i in range(PIECES):
        part = slice(i * rows // PIECES, (i + 1) * rows // PIECES)
        held[part] = (own_ref[part] + arrived_ref[part].astype(F32)) * (1.0 / count)
        target = out.at[0, part, way * half : (way + 1) * half]
        copies.append(pltpu.make_async_copy(held.at[part], target, sems.at[i]))
        copies[-1].start()
    for copy in copies:
        copy.wait()


def last_call(name, count, arrived, own, after):
    rows, half = own[0].shape
    out = []
    for way in range(2):
        out = [
            pl.pallas_call(
                functools.partial(last_kernel, way, count),
                in_specs=[WHOLE] * 2
                + [pl.BlockSpec(memory_space=pltpu.HBM)] * len(out)
                + [LATER] * len(after),
                out_specs=pl.BlockSpec(memory_space=pltpu.HBM),
                out_shape=pltpu.HBM((1, rows, 2 * half), F32),
                input_output_aliases={2: 0} if out else {},
                scratch_shapes=[pltpu.VMEM((rows, half), F32), pltpu.SemaphoreType.DMA((PIECES,))],
                compiler_params=params(),
                name=name,
            )(arrived[way], own[way], *(in_hbm(a) for a in out), *after)
        ]
        after = []
    return out[0]


def ring_step(name, step, count, shape, lefts, rights, arrived, after=(), dtype=BF16):
    blocks = [block for group in rights for block in group]
    inputs = [*lefts, *blocks, *arrived]
    return pl.pallas_call(
        functools.partial(step_kernel, [len(group) for group in rights], len(arrived), step, count),
        in_specs=[WHOLE] * len(inputs) + [LATER] * len(after),
        out_specs=[WHOLE] * 2,
        out_shape=[jax.ShapeDtypeStruct(shape, dtype)] * 2,
        compiler_params=params(),
        name=name,
    )(*inputs, *after)


def per_device(tokens, out_grad, gate_prob, expert_id, up_weight, down_weight):
    count, width = tokens.shape
    inner = up_weight.shape[2]
    peers = lax.axis_size("expert")
    experts = peers * up_weight.shape[0]
    capacity = 2 * count // experts
    ring = lax.axis_size("dp")
    sources = [[(i, i ^ k) for i in range(peers)] for k in range(peers)]
    forward = ring_pairs(ring)
    backward = [(b, a) for a, b in forward]

    def exchange(outs, reach):
        return {k: lax.ppermute(outs[k], "expert", sources[k]) for k in reach}

    near, far = range(1, peers // 2), range(peers // 2, peers)
    hbm = pl.BlockSpec(memory_space=pltpu.HBM)
    across = [(i, i ^ peers // 2) for i in range(peers)]
    tokens_across = lax.ppermute(tokens, "expert", across)
    id_across = lax.ppermute(expert_id.reshape(1, count), "expert", across)

    block_shape = jax.ShapeDtypeStruct((capacity, width), BF16)
    slot, *packed = pl.pallas_call(
        functools.partial(pack_kernel, experts, capacity, peers // 2),
        in_specs=[hbm] * 4,
        out_specs=[WHOLE] * (1 + peers // 2 + peers),
        out_shape=[jax.ShapeDtypeStruct((1, count), jnp.int32)]
        + [block_shape] * (peers // 2 + peers),
        scratch_shapes=[
            pltpu.VMEM((count,), jnp.int32),
            pltpu.VMEM((count,), BF16),
            pltpu.VMEM((count, width), BF16),
            pltpu.VMEM((count, width), BF16),
            pltpu.SemaphoreType.DMA((4,)),
        ],
        compiler_params=params(),
        name="pack",
    )(*(in_hbm(a) for a in (expert_id, gate_prob, out_grad, tokens)))
    feat_out, grad_out = packed[: peers // 2], packed[peers // 2 :]
    grad_in = {0: grad_out[0], **exchange(grad_out, far), **exchange(grad_out, near)}
    feat_in = {0: feat_out[0], **exchange(feat_out, near)}
    groups = [[0, *near], [peers // 2], [*far][1:]]
    groups = [group for group in groups if group]
    scaleds = [[grad_in[k] for k in group] for group in groups]
    hiddens, pre_grads, sums = [], [], []

    def add_hidden(blocks, after=()):
        hiddens.append(hidden_call(blocks, up_weight, after))
        return [hiddens[-1][1]]

    def add_pre_grad(after=()):
        group = len(pre_grads)
        _, hidden, _, slope = hiddens[group]
        pre, total = pre_grad_call(scaleds[group], down_weight, hidden, slope, after)
        pre_grads.append([pre])
        sums.append(total)
        return [total]

    add_hidden([feat_in[k] for k in groups[0]])
    after = add_pre_grad()
    across_out = pl.pallas_call(
        functools.partial(repack_kernel, experts, capacity),
        in_specs=[WHOLE, WHOLE, LATER],
        out_specs=[WHOLE] * (peers // 2),
        out_shape=[block_shape] * (peers // 2),
        compiler_params=params(),
        name="repack",
    )(id_across, tokens_across, *after)
    across_in = exchange(across_out, near)
    after = add_hidden(across_out[:1])
    if len(groups) > 2:
        after = add_pre_grad(after)
        after = add_hidden([across_in[k] for k in near], after)
    flip_feats = [part[0] for part in hiddens]
    flip_hiddens = [part[2] for part in hiddens]
    down_shape = (inner // ring, width // 2)
    up_shape = (width // ring, inner // 2)
    down_in = ring_step(
        "down_early",
        1,
        ring,
        down_shape,
        flip_hiddens[:-1],
        scaleds[:-1],
        [],
        after,
        F32,
    )

    def send(pair):
        return [lax.ppermute(pair[0], "dp", forward), lax.ppermute(pair[1], "dp", backward)]

    turn = 1 if ring < 8 else 2
    span = min(4, ring - turn)
    returns = [*far, *near, 0]
    feat_back = {}
    up_in, after, landed = [], [], []
    for step in range(1, ring):
        late = slice(-1, None) if step == 1 else slice(None)
        down = ring_step(
            "down_step",
                step,
            ring,
            down_shape,
            flip_hiddens[late],
            scaleds[late],
            down_in,
            after,
        )
        down_in = send(down)
        after = [*down]
        if step == 1:
            after = add_pre_grad(after)
        up = ring_step(
            "up_step", step, ring, up_shape, flip_feats, pre_grads, up_in, after
        )
        up_in = send(up)
        after = [*up] + landed
        landed = []
        first = (step - turn) * len(returns) // span
        stop = (step - turn + 1) * len(returns) // span
        for k in returns[max(first, 0) : max(stop, 0)]:
            group = [k in members for members in groups].index(True)
            block = feat_grad_call(
                pre_grads[group][0],
                up_weight,
                sums[group],
                groups[group].index(k),
                capacity,
                after,
            )
            after = [block]
            feat_back[k] = lax.ppermute(block, "expert", sources[k]) if k else block
            landed.append(feat_back[k])
        if step == max(ring - 2, 1):
            down_last = ring_step(
                "down_own",
                        ring,
                ring,
                down_shape,
                flip_hiddens,
                scaleds,
                [],
                after,
                F32,
            )
            up_last = ring_step(
                "up_own",
                        ring,
                ring,
                up_shape,
                flip_feats,
                pre_grads,
                [],
                down_last[:1],
                F32,
            )
            after = up_last[:1]
    down = last_call("down_last", ring, down_in, down_last, [])
    up = last_call("up_last", ring, up_in, up_last, [in_hbm(down)])
    tokens_grad, gate_sums = pl.pallas_call(
        functools.partial(unpack_kernel, capacity, width, peers),
        in_specs=[WHOLE] * (1 + peers) + [LATER] * len(after),
        out_specs=[WHOLE] * 2,
        out_shape=[
            jax.ShapeDtypeStruct((count, width), BF16),
            jax.ShapeDtypeStruct((count, LANES), F32),
        ],
        compiler_params=params(),
        name="unpack",
    )(slot, *(feat_back[k] for k in range(peers)), *after)
    gate_result = ((gate_sums[:, 0] + gate_sums[:, 1]) / gate_prob.astype(F32)).astype(BF16)
    return (tokens_grad, gate_result, up, down)


def solution(mesh):
    return jax.shard_map(
        per_device,
        mesh=mesh,
        in_specs=(
            P(("dp", "expert"), None),
            P(("dp", "expert"), None),
            P(("dp", "expert")),
            P(("dp", "expert")),
            P("expert", None, None),
            P("expert", None, None),
        ),
        out_specs=(
            P(("dp", "expert"), None),
            P(("dp", "expert")),
            P("expert", "dp", None),
            P("expert", "dp", None),
        ),
        check_vma=False,
    )
```

```python
import functools

import jax
import jax.numpy as jnp
from jax import lax
from jax.experimental import pallas as pl
from jax.experimental.pallas import tpu as pltpu
from jax.sharding import PartitionSpec as P

SQRT_HALF = 0.7071067811865476
INV_ROOT_TAU = 0.3989422804014327
LANES = 128
VMEM_LIMIT = 16 * 1024 * 1024
F32 = jnp.float32
BF16 = jnp.bfloat16
WHOLE = pl.BlockSpec(memory_space=pltpu.VMEM)
LATER = pl.BlockSpec(memory_space=pl.ANY)


def in_hbm(array):
    return pltpu.with_memory_space_constraint(array, pltpu.HBM)


def params(*semantics):
    return pltpu.CompilerParams(
        vmem_limit_bytes=VMEM_LIMIT, dimension_semantics=semantics or None
    )


def dot(left, right, left_dim, right_dim):
    return lax.dot_general(
        left, right, (((left_dim,), (right_dim,)), ((), ())), preferred_element_type=F32
    )


def slot_row(id_row, experts, capacity, me):
    count = id_row.shape[1]
    expert = lax.broadcasted_iota(jnp.int32, (max(experts, 8), count), 0)
    chosen = expert == id_row
    earlier = lax.broadcasted_iota(jnp.int32, (count, count), 0) < lax.broadcasted_iota(
        jnp.int32, (count, count), 1
    )
    before = dot(
        jnp.where(chosen, 1.0, 0.0).astype(BF16), jnp.where(earlier, 1.0, 0.0).astype(BF16), 1, 0
    )
    position = jnp.sum(jnp.where(chosen, before, 0.0), axis=0, keepdims=True).astype(jnp.int32)
    return (id_row ^ me) * capacity + position


def pick_rows(slot, block, capacity, value):
    row = lax.broadcasted_iota(jnp.int32, (capacity, slot.shape[1]), 0) + block * capacity
    return jnp.where(row == slot, value, 0.0).astype(BF16)


def pack_kernel(experts, capacity, near, *refs):
    sources, refs = refs[:4], refs[4:]
    slot_ref, outs = refs[0], refs[1:-5]
    held, sems = refs[-5:-1], refs[-1]
    copies = [
        pltpu.make_async_copy(source, target, sems.at[i])
        for i, (source, target) in enumerate(zip(sources, held))
    ]
    for copy in copies:
        copy.start()
    id_ref, gate_ref, grad_ref, tokens_ref = held
    copies[0].wait()
    count = id_ref.shape[0]
    slot = slot_row(id_ref[...].reshape(1, count), experts, capacity, lax.axis_index("expert"))
    slot_ref[...] = slot
    for copy in copies[1:]:
        copy.wait()
    gate = gate_ref[...].astype(F32).reshape(1, count)
    for block, out in enumerate(outs[near:]):
        out[...] = dot(pick_rows(slot, block, capacity, gate), grad_ref[...], 1, 0).astype(BF16)
    for block, out in enumerate(outs[:near]):
        out[...] = dot(pick_rows(slot, block, capacity, 1.0), tokens_ref[...], 1, 0).astype(BF16)


def repack_kernel(experts, capacity, id_ref, tokens_ref, _, *outs):
    slot = slot_row(id_ref[...], experts, capacity, lax.axis_index("expert"))
    for block, out in enumerate(outs):
        out[...] = dot(pick_rows(slot, block, capacity, 1.0), tokens_ref[...], 1, 0).astype(BF16)


def unpack_kernel(capacity, width, peers, slot_ref, *refs):
    blocks, (feat_ref, gate_ref) = refs[:peers], refs[-2:]
    slot = slot_ref[...]
    count = slot.shape[1]
    total = None
    for block, ref in enumerate(blocks):
        row = lax.broadcasted_iota(jnp.int32, (capacity, count), 0) + block * capacity
        pick = jnp.where(row == slot, 1.0, 0.0).astype(BF16)
        part = dot(pick, ref[...], 0, 0)
        total = part if total is None else total + part
    feat_ref[...] = total[:, :width].astype(BF16)
    gate_ref[...] = total[:, width:]


def call(body, inputs, out_shape, name, after=()):
    return pl.pallas_call(
        body,
        in_specs=[WHOLE] * len(inputs) + [LATER] * len(after),
        out_specs=[WHOLE] * len(out_shape),
        out_shape=[jax.ShapeDtypeStruct(*s) for s in out_shape],
        compiler_params=params(),
        name=name,
    )(*inputs, *after)


def hidden_kernel(peers, tiles, *refs):
    blocks, up_ref = refs[:peers], refs[peers]
    flip_feat_ref, hidden_ref, flip_hidden_ref, slope_ref = refs[-4:]
    feat = jnp.concatenate([ref[...] for ref in blocks], axis=0)
    flip_feat_ref[...] = feat.T
    tile = up_ref.shape[2] // tiles
    for i in range(tiles):
        part = slice(i * tile, (i + 1) * tile)
        pre_act = dot(feat, up_ref[0, :, part], 1, 0)
        cdf = 0.5 * (1.0 + lax.erf(pre_act * SQRT_HALF))
        hidden = (pre_act * cdf).astype(BF16)
        hidden_ref[:, part] = hidden
        flip_hidden_ref[part, :] = hidden.T
        slope = cdf + pre_act * jnp.exp(-0.5 * pre_act * pre_act) * INV_ROOT_TAU
        slope_ref[:, part] = slope.astype(BF16)


def hidden_call(blocks, up_weight, after=()):
    _, width, inner = up_weight.shape
    rows = len(blocks) * blocks[0].shape[0]
    return call(
        functools.partial(hidden_kernel, len(blocks), 8),
        [*blocks, up_weight],
        [
            ((width, rows), BF16),
            ((rows, inner), BF16),
            ((inner, rows), BF16),
            ((rows, inner), BF16),
        ],
        "hidden",
        after,
    )


def pre_grad_kernel(peers, tiles, *refs):
    blocks = refs[:peers]
    down_ref, hidden_ref, slope_ref = refs[peers : peers + 3]
    pre_ref, sum_ref = refs[-2:]
    scaled = jnp.concatenate([ref[...] for ref in blocks], axis=0)
    tile = down_ref.shape[1] // tiles
    total = 0.0
    for i in range(tiles):
        part = slice(i * tile, (i + 1) * tile)
        hidden_grad = dot(scaled, down_ref[0, part, :], 1, 1)
        pre_ref[:, part] = (hidden_grad * slope_ref[:, part].astype(F32)).astype(BF16)
        product = hidden_grad * hidden_ref[:, part].astype(F32)
        for j in range(tile // LANES):
            total += product[:, j * LANES : (j + 1) * LANES]
    sum_ref[...] = jnp.broadcast_to(jnp.sum(total, axis=1, keepdims=True), sum_ref.shape)


def pre_grad_call(blocks, down_weight, hidden, slope, after=()):
    _, inner, width = down_weight.shape
    rows = len(blocks) * blocks[0].shape[0]
    return call(
        functools.partial(pre_grad_kernel, len(blocks), 8),
        [*blocks, down_weight, hidden, slope],
        [((rows, inner), BF16), ((rows, LANES), F32)],
        "pre_grad",
        after,
    )


def feat_grad_kernel(block, pre_ref, up_ref, sum_ref, *refs):
    out = refs[-1]
    capacity = out.shape[0]
    part = slice(block * capacity, (block + 1) * capacity)
    width = up_ref.shape[1]
    out[:, :width] = dot(pre_ref[part, :], up_ref[0], 1, 1).astype(BF16)
    total = sum_ref[part, :]
    high = total.astype(BF16).astype(F32)
    lane = lax.broadcasted_iota(jnp.int32, total.shape, 1)
    out[:, width:] = jnp.where(lane == 0, high, total - high).astype(BF16)


def feat_grad_call(pre_grad, up_weight, sums, block, capacity, after=()):
    shape = (capacity, up_weight.shape[1] + LANES)
    return call(
        functools.partial(feat_grad_kernel, block),
        [pre_grad, up_weight, sums],
        [(shape, BF16)],
        "feat_grad",
        after,
    )[0]


def ring_chunk(step, count):
    index = lax.axis_index("dp")
    half = lax.div(index, 2)
    place = jnp.where(lax.rem(index, 2) == 0, count - 1 - half, half)
    chunks = []
    for move in (count - step, step):
        position = lax.rem(place + move, count)
        mirror = 2 * (count - 1 - position)
        chunks.append(jnp.where(position < count // 2, 2 * position + 1, mirror))
    return chunks


def ring_pairs(count):
    half = count // 2
    ring = [2 * p + 1 if p < half else 2 * (count - 1 - p) for p in range(count)]
    return [(ring[p], ring[(p + 1) % count]) for p in range(count)]


def step_kernel(parts, arrivals, step, count, *refs):
    groups = len(parts)
    lefts, refs = refs[:groups], refs[groups:]
    rights, refs = refs[: sum(parts)], refs[sum(parts) :]
    totals = [0.0, 0.0]
    chunks = ring_chunk(step, count) if groups else None
    for i, ref in enumerate(refs[:arrivals]):
        totals[i % 2] += ref[...].astype(F32)
    for left, blocks in zip(lefts, parts):
        right = [ref[...] for ref in rights[:blocks]]
        right = right[0] if blocks == 1 else jnp.concatenate(right, axis=0)
        rights = rights[blocks:]
        half = right.shape[1] // 2
        rows = left.shape[0] // count
        for way in range(2):
            start = pl.multiple_of(chunks[way] * rows, rows)
            totals[way] += dot(
                left[pl.ds(start, rows), :], right[:, way * half : (way + 1) * half], 1, 0
            )
    for way, out in enumerate(refs[-2:]):
        out[...] = totals[way].astype(out.dtype)


def last_kernel(way, count, arrived_ref, own_ref, *refs):
    out, held, sem = refs[-3:]
    half = held.shape[1]
    held[...] = (own_ref[...] + arrived_ref[...].astype(F32)) * (1.0 / count)
    copy = pltpu.make_async_copy(held, out.at[0, :, way * half : (way + 1) * half], sem)
    copy.start()
    copy.wait()


def last_call(name, count, arrived, own, after):
    rows, half = own[0].shape
    out = []
    for way in range(2):
        out = [
            pl.pallas_call(
                functools.partial(last_kernel, way, count),
                in_specs=[WHOLE] * 2
                + [pl.BlockSpec(memory_space=pltpu.HBM)] * len(out)
                + [LATER] * len(after),
                out_specs=pl.BlockSpec(memory_space=pltpu.HBM),
                out_shape=pltpu.HBM((1, rows, 2 * half), F32),
                input_output_aliases={2: 0} if out else {},
                scratch_shapes=[pltpu.VMEM((rows, half), F32), pltpu.SemaphoreType.DMA],
                compiler_params=params(),
                name=name,
            )(arrived[way], own[way], *(in_hbm(a) for a in out), *after)
        ]
        after = []
    return out[0]


def ring_step(name, step, count, shape, lefts, rights, arrived, after=(), dtype=BF16):
    blocks = [block for group in rights for block in group]
    inputs = [*lefts, *blocks, *arrived]
    return pl.pallas_call(
        functools.partial(step_kernel, [len(group) for group in rights], len(arrived), step, count),
        in_specs=[WHOLE] * len(inputs) + [LATER] * len(after),
        out_specs=[WHOLE] * 2,
        out_shape=[jax.ShapeDtypeStruct(shape, dtype)] * 2,
        compiler_params=params(),
        name=name,
    )(*inputs, *after)


def per_device(tokens, out_grad, gate_prob, expert_id, up_weight, down_weight):
    count, width = tokens.shape
    inner = up_weight.shape[2]
    peers = lax.axis_size("expert")
    experts = peers * up_weight.shape[0]
    capacity = 2 * count // experts
    ring = lax.axis_size("dp")
    sources = [[(i, i ^ k) for i in range(peers)] for k in range(peers)]
    forward = ring_pairs(ring)
    backward = [(b, a) for a, b in forward]

    def exchange(outs, reach):
        return {k: lax.ppermute(outs[k], "expert", sources[k]) for k in reach}

    near, far = range(1, peers // 2), range(peers // 2, peers)
    hbm = pl.BlockSpec(memory_space=pltpu.HBM)
    across = [(i, i ^ peers // 2) for i in range(peers)]
    tokens_across = lax.ppermute(tokens, "expert", across)
    id_across = lax.ppermute(expert_id.reshape(1, count), "expert", across)

    block_shape = jax.ShapeDtypeStruct((capacity, width), BF16)
    slot, *packed = pl.pallas_call(
        functools.partial(pack_kernel, experts, capacity, peers // 2),
        in_specs=[hbm] * 4,
        out_specs=[WHOLE] * (1 + peers // 2 + peers),
        out_shape=[jax.ShapeDtypeStruct((1, count), jnp.int32)]
        + [block_shape] * (peers // 2 + peers),
        scratch_shapes=[
            pltpu.VMEM((count,), jnp.int32),
            pltpu.VMEM((count,), BF16),
            pltpu.VMEM((count, width), BF16),
            pltpu.VMEM((count, width), BF16),
            pltpu.SemaphoreType.DMA((4,)),
        ],
        compiler_params=params(),
        name="pack",
    )(*(in_hbm(a) for a in (expert_id, gate_prob, out_grad, tokens)))
    feat_out, grad_out = packed[: peers // 2], packed[peers // 2 :]
    grad_in = {0: grad_out[0], **exchange(grad_out, far), **exchange(grad_out, near)}
    feat_in = {0: feat_out[0], **exchange(feat_out, near)}
    groups = [[0, *near], [peers // 2], [*far][1:]]
    groups = [group for group in groups if group]
    scaleds = [[grad_in[k] for k in group] for group in groups]
    hiddens, pre_grads, sums = [], [], []

    def add_hidden(blocks, after=()):
        hiddens.append(hidden_call(blocks, up_weight, after))
        return [hiddens[-1][1]]

    def add_pre_grad(after=()):
        group = len(pre_grads)
        _, hidden, _, slope = hiddens[group]
        pre, total = pre_grad_call(scaleds[group], down_weight, hidden, slope, after)
        pre_grads.append([pre])
        sums.append(total)
        return [total]

    add_hidden([feat_in[k] for k in groups[0]])
    after = add_pre_grad()
    across_out = pl.pallas_call(
        functools.partial(repack_kernel, experts, capacity),
        in_specs=[WHOLE, WHOLE, LATER],
        out_specs=[WHOLE] * (peers // 2),
        out_shape=[block_shape] * (peers // 2),
        compiler_params=params(),
        name="repack",
    )(id_across, tokens_across, *after)
    across_in = exchange(across_out, near)
    after = add_hidden(across_out[:1])
    if len(groups) > 2:
        after = add_pre_grad(after)
        after = add_hidden([across_in[k] for k in near], after)
    flip_feats = [part[0] for part in hiddens]
    flip_hiddens = [part[2] for part in hiddens]
    down_shape = (inner // ring, width // 2)
    up_shape = (width // ring, inner // 2)
    down_in = ring_step(
        "down_early",
        1,
        ring,
        down_shape,
        flip_hiddens[:-1],
        scaleds[:-1],
        [],
        after,
        F32,
    )

    def send(pair):
        return [lax.ppermute(pair[0], "dp", forward), lax.ppermute(pair[1], "dp", backward)]

    turn = 1 if ring < 8 else 2
    span = min(4, ring - turn)
    returns = [*far, *near, 0]
    feat_back = {}
    up_in, after, landed = [], [], []
    for step in range(1, ring):
        late = slice(-1, None) if step == 1 else slice(None)
        down = ring_step(
            "down_step",
                step,
            ring,
            down_shape,
            flip_hiddens[late],
            scaleds[late],
            down_in,
            after,
        )
        down_in = send(down)
        after = [*down]
        if step == 1:
            after = add_pre_grad(after)
        up = ring_step(
            "up_step", step, ring, up_shape, flip_feats, pre_grads, up_in, after
        )
        up_in = send(up)
        after = [*up] + landed
        landed = []
        first = (step - turn) * len(returns) // span
        stop = (step - turn + 1) * len(returns) // span
        for k in returns[max(first, 0) : max(stop, 0)]:
            group = [k in members for members in groups].index(True)
            block = feat_grad_call(
                pre_grads[group][0],
                up_weight,
                sums[group],
                groups[group].index(k),
                capacity,
                after,
            )
            after = [block]
            feat_back[k] = lax.ppermute(block, "expert", sources[k]) if k else block
            landed.append(feat_back[k])
        if step == max(ring - 2, 1):
            down_last = ring_step(
                "down_own",
                        ring,
                ring,
                down_shape,
                flip_hiddens,
                scaleds,
                [],
                after,
                F32,
            )
            up_last = ring_step(
                "up_own",
                        ring,
                ring,
                up_shape,
                flip_feats,
                pre_grads,
                [],
                down_last[:1],
                F32,
            )
            after = up_last[:1]
    down = last_call("down_last", ring, down_in, down_last, [])
    up = last_call("up_last", ring, up_in, up_last, [in_hbm(down)])
    tokens_grad, gate_sums = pl.pallas_call(
        functools.partial(unpack_kernel, capacity, width, peers),
        in_specs=[WHOLE] * (1 + peers) + [LATER] * len(after),
        out_specs=[WHOLE] * 2,
        out_shape=[
            jax.ShapeDtypeStruct((count, width), BF16),
            jax.ShapeDtypeStruct((count, LANES), F32),
        ],
        compiler_params=params(),
        name="unpack",
    )(slot, *(feat_back[k] for k in range(peers)), *after)
    gate_result = ((gate_sums[:, 0] + gate_sums[:, 1]) / gate_prob.astype(F32)).astype(BF16)
    return (tokens_grad, gate_result, up, down)


def solution(mesh):
    return jax.shard_map(
        per_device,
        mesh=mesh,
        in_specs=(
            P(("dp", "expert"), None),
            P(("dp", "expert"), None),
            P(("dp", "expert")),
            P(("dp", "expert")),
            P("expert", None, None),
            P("expert", None, None),
        ),
        out_specs=(
            P(("dp", "expert"), None),
            P(("dp", "expert")),
            P("expert", "dp", None),
            P("expert", "dp", None),
        ),
        check_vma=False,
    )
```
